32 devices in a mesh: groups: 2 (over x), qry: 16 (over z, y, core).
Axes of the slice: x: 2, y: 2, z: 4, core: 2. Of those that a mesh axis runs over, the one named last changes fastest.
Arguments:
- queries: bfloat16 [32768, 128], P(('groups', 'qry')), parts along dimension 0, may hold values from -1.5 to 1.5
- vectors: bfloat16 [4096, 128], P(('groups', 'qry')), parts along dimension 0, may hold values from -3 to 3
- decoded: bfloat16 [4096, 128], P(('groups', 'qry')), parts along dimension 0, may hold values from -3 to 3
- mask: int32 [128, 8], P(('groups', 'qry')), parts along dimension 0, may hold values from 0 to 1, as said below
Outputs:
- grad_queries: float32 [32768, 128], P(('groups', 'qry')), parts along dimension 0
- grad_vectors: float32 [4096, 128], P(('groups', 'qry')), parts along dimension 0
- grad_decoded: float32 [4096, 128], P(('groups', 'qry')), parts along dimension 0
The draws below stay inside these ranges and needn't reach their ends.
There are 2 independent parts, one for each index of `groups`. The reference program is written for one: setup_inputs(seed, part) draws one part's arguments, and reference() takes and returns one part's arrays. A program takes and returns all parts, laid end to end along the dimension named above; each array names one. Nothing has to cross between parts.
Inputs may be any that keep to these rules, and one draw needn't show every extreme that they name: mask[b, k] is 1 where query block b and vector block k are a sampled pair; how many pairs a query block samples differs from block to block.
All inputs are finite; a program needn't handle non-finite values.
Results may differ from the reference program's by a relative error of at most 0.0012.
Values may be sent and summed in bfloat16 or wider, within the bound.
No kernel may reach another device: no remote copies, remote signals or barrier semaphores. Data moves between devices by JAX's collectives and lax.ppermute only.
A program may use at most 256 MiB of HBM per device.

```python
import math
import jax
import jax.numpy as jnp
from jax import lax

D = 128
BLK = 256
NQ = 16384
NV = 2048
NQB = 64
NVB = 8


def draw_mask(key, part):
    first, second = jax.random.split(jax.random.fold_in(key, 17))
    rates = jax.random.randint(first, (NQB, 1), 1, 9)
    levels = jax.random.randint(second, (NQB, NVB), 0, 8)
    return (levels < rates).astype(jnp.int32)


def block_scale(stream_key, dims, pieces, smallest, high):
    level = 1.0
    for dim, shards_of in pieces:
        draws = jax.random.uniform(jax.random.fold_in(jax.random.fold_in(stream_key, 6), dim), (shards_of,), jnp.float32, smallest / len(pieces), high / len(pieces))
        level = level * jnp.repeat(jnp.exp(draws), dims[dim] // shards_of).reshape((-1,) + (1,) * (len(dims) - 1 - dim))
    return level


def scatter_about(key, extent, deviation, most, shards=(), held_as=jnp.bfloat16):
    entries = deviation * jax.random.normal(key, extent, jnp.float32)
    if shards:
        entries = entries * block_scale(key, extent, shards, -0.22, 0.18)
    return jnp.clip(entries, -most, most).astype(held_as)


def setup_inputs(seed: int = 0, part: int = 0) -> dict:
    streams_of = jax.random.split(jax.random.key(seed), 5)
    part_splits = jax.random.split(jax.random.fold_in(streams_of[4], part), 5)
    queries = scatter_about(part_splits[0], (NQ, D), 0.25, 1.5, ((0, 16),))
    vectors = scatter_about(part_splits[1], (NV, D), 0.5, 3.0, ((0, 16),))
    decoded = scatter_about(part_splits[2], (NV, D), 0.5, 3.0, ((0, 16),))
    mask = draw_mask(jax.random.fold_in(jax.random.fold_in(streams_of[4], part), 71), part)
    return {"queries": queries, "vectors": vectors, "decoded": decoded, "mask": mask}


def block_grads(query_rows, vec_rows, dec_rows, live, scale):
    score = jnp.dot(query_rows, vec_rows.T, preferred_element_type=jnp.float32)
    error = score - jnp.dot(query_rows, dec_rows.T, preferred_element_type=jnp.float32)
    sig = jax.nn.sigmoid(score)
    pos_weight = (scale * live * (sig * (1.0 - sig) * error * error + 2.0 * sig * error)).astype(jnp.bfloat16)
    neg_weight = (scale * live * 2.0 * sig * error).astype(jnp.bfloat16)
    grad_q = jnp.dot(pos_weight, vec_rows, preferred_element_type=jnp.float32) - jnp.dot(neg_weight, dec_rows, preferred_element_type=jnp.float32)
    grad_v = jnp.dot(pos_weight.T, query_rows, preferred_element_type=jnp.float32)
    grad_d = -jnp.dot(neg_weight.T, query_rows, preferred_element_type=jnp.float32)
    return (grad_q, grad_v, grad_d)

def reference(queries, vectors, decoded, mask):
    scale = 1.0 / math.sqrt(NV)
    query_blocks = queries.reshape(NQB, BLK, D)

    def visit(carry, items):
        grad_vec, grad_dec = carry
        query_rows, mask_row = items
        live_row = jnp.repeat(mask_row.astype(jnp.float32), BLK)
        live = jnp.broadcast_to(live_row[None, :], (BLK, NV))
        grad_q, grad_v, grad_d = block_grads(query_rows, vectors, decoded, live, scale)
        return ((grad_vec + grad_v, grad_dec + grad_d), grad_q)
    init = (jnp.zeros((NV, D), jnp.float32), jnp.zeros((NV, D), jnp.float32))
    (grad_vec, grad_dec), grad_q = lax.scan(visit, init, (query_blocks, mask))
    return (grad_q.reshape(NQ, D), grad_vec, grad_dec)
```

```python
import math

import jax
import jax.numpy as jnp
from jax import lax
from jax.experimental import pallas as pl
from jax.experimental.pallas import tpu as pltpu
from jax.sharding import PartitionSpec as P

BLK = 256
LOG2E = 1.4426950408889634
VMEM = pl.BlockSpec(memory_space=pltpu.VMEM)
F32 = jnp.float32


def params(mib):
    return pltpu.CompilerParams(vmem_limit_bytes=mib << 20)


def pack_kernel(q_ref, v_ref, d_ref, m_ref, qm_ref, vd_ref):
    rows = q_ref.shape[0]
    local_v = v_ref.shape[0]
    qm_ref[0:rows, :] = q_ref[...]
    tail = jnp.zeros((qm_ref.shape[0] - rows, q_ref.shape[1]), F32)
    blocks, cols = m_ref.shape
    padded = jnp.concatenate(
        [m_ref[...].astype(F32), jnp.zeros((blocks, q_ref.shape[1] - cols), F32)], axis=1
    )
    tail = jnp.concatenate([padded, tail[blocks:]], axis=0)
    qm_ref[rows:, :] = tail.astype(jnp.bfloat16)
    vd_ref[0:local_v, :] = v_ref[...]
    vd_ref[local_v:, :] = d_ref[...]


def grads_kernel(rows, blocks, chunks, local_v, scale, *refs):
    qm_refs, vd_refs = refs[:4], refs[4 : 4 + chunks]
    gq_refs, gv_ref = refs[4 + chunks : 8 + chunks], refs[8 + chunks]
    w_ref, live_ref = refs[9 + chunks :]
    me = lax.axis_index("qry")
    wide = 2 * local_v
    group = min(chunks, 4)
    for s in range(chunks):
        w_ref[s * wide : (s + 1) * wide, :] = vd_refs[s][...]
    pad = qm_refs[0].shape[0] - rows
    lanes = lax.broadcasted_iota(jnp.int32, (pad, 128), 1)
    for t in range(4):
        flags = qm_refs[t][rows:, :].astype(F32)
        for s in range(chunks):
            col = (jnp.bitwise_xor(me, 4 * s) * local_v) // BLK
            flag = jnp.sum(jnp.where(lanes == col, flags, 0.0), axis=1, keepdims=True)
            live_ref[s, t * pad : (t + 1) * pad, :] = jnp.broadcast_to(
                flag * (-2.0 * scale), (pad, 128)
            )
    gv_ref[...] = jnp.zeros_like(gv_ref)

    def tile(t, r0, height, g):
        q = qm_refs[t][pl.ds(r0, height), :]
        w = w_ref[pl.ds(g * group * wide, group * wide), :]
        both = lax.dot_general(q, w, (((1,), (1,)), ((), ())), preferred_element_type=F32)
        row_blocks = []
        for b in range(height // BLK):
            weights = []
            for c in range(group):
                score = both[b * BLK : (b + 1) * BLK, c * wide : c * wide + local_v]
                error = score - both[b * BLK : (b + 1) * BLK, c * wide + local_v : (c + 1) * wide]
                m = live_ref[g * group + c, pl.ds(t * pad + r0 // BLK + b, 1), :]
                sig = 1.0 / (1.0 + jnp.exp2(score * (-LOG2E)))
                neg = (error * m) * sig
                pos = neg * (error * (0.5 * sig - 0.5) - 1.0)
                weights += [pos.astype(jnp.bfloat16), neg.astype(jnp.bfloat16)]
            row_blocks.append(jnp.concatenate(weights, axis=1))
        weights = jnp.concatenate(row_blocks, axis=0)
        part = jnp.dot(weights, w, preferred_element_type=F32)
        if chunks == group:
            gq_refs[t][pl.ds(r0, height), :] = part
        else:
            gq_refs[t][pl.ds(r0, height), :] = part + jnp.where(
                g == 0, 0.0, gq_refs[t][pl.ds(r0, height), :]
            )
        gv_ref[g] += jnp.dot(q.T, weights, preferred_element_type=F32)

    height = 2 * BLK if rows % (2 * BLK) == 0 else BLK
    for t in range(4):
        if chunks == group:
            for i in range(rows // height):
                tile(t, i * height, height, 0)
        else:

            def step(n, carry, t=t):
                g = n // (rows // height)
                r0 = pl.multiple_of((n % (rows // height)) * height, height)
                tile(t, r0, height, g)
                return carry

            lax.fori_loop(0, (chunks // group) * (rows // height), step, 0)


def core_sum_kernel(own_ref, y_ref, got_ref, own_out, y_out):
    rows = own_ref.shape[0]
    own_out[...] = own_ref[...] + got_ref[0:rows, :]
    y_out[...] = y_ref[...] + got_ref[rows:, :]


def finish_kernel(n, *refs):
    own_ref, got_ref = refs[:2]
    terms = refs[2 : 2 + n]
    gq_out, gv_out, gd_out = refs[2 + n :]
    gq_out[...] = own_ref[...] + got_ref[...]
    total = terms[0][...]
    for term in terms[1:]:
        total = total + term[...]
    local_v = gv_out.shape[0]
    gv_out[...] = total[:, :local_v].T
    gd_out[...] = total[:, local_v:].T


def body(queries, vectors, decoded, mask):
    rows, dim = queries.shape
    local_v = vectors.shape[0]
    blocks, blocks_v = mask.shape
    n = lax.axis_size("qry")
    chunks = n // 4
    wide = 2 * local_v
    scale = 1.0 / math.sqrt(local_v * n)
    pad = -(-blocks // 16) * 16
    bf = jnp.bfloat16

    def swap(x, bit):
        return lax.ppermute(x, "qry", [(i, i ^ bit) for i in range(n)])

    qm, vd = pl.pallas_call(
        pack_kernel,
        out_shape=(
            jax.ShapeDtypeStruct((rows + pad, dim), bf),
            jax.ShapeDtypeStruct((wide, dim), bf),
        ),
        in_specs=[VMEM] * 4,
        out_specs=(VMEM, VMEM),
        compiler_params=params(8),
        name="pack",
    )(queries, vectors, decoded, mask)
    qm_y = swap(qm, 2)
    vds = [vd] + [swap(vd, 4 * s) for s in range(1, chunks)]
    qm_c = swap(qm, 1)
    qm_yc = swap(qm_y, 1)
    group = min(chunks, 4)
    row_out = jax.ShapeDtypeStruct((rows, dim), F32)
    gq_own, gq_c, gq_y, gq_yc, gv = pl.pallas_call(
        lambda *refs: grads_kernel(rows, blocks, chunks, local_v, scale, *refs),
        out_shape=(row_out,) * 4
        + (jax.ShapeDtypeStruct((chunks // group, dim, group * wide), F32),),
        in_specs=[VMEM] * (4 + chunks),
        out_specs=(VMEM,) * 5,
        scratch_shapes=[
            pltpu.VMEM((chunks * wide, dim), bf),
            pltpu.VMEM((chunks, 4 * pad, 128), F32),
        ],
        compiler_params=params(40),
        name="grads",
    )(qm, qm_c, qm_y, qm_yc, *vds)
    terms = [
        gv[s // group, :, (s % group) * wide : (s % group + 1) * wide] for s in range(chunks)
    ]
    got_c = swap(jnp.concatenate([gq_c, gq_yc], axis=0), 1)
    gq_own, gq_y = pl.pallas_call(
        core_sum_kernel,
        out_shape=(row_out,) * 2,
        in_specs=[VMEM] * 3,
        out_specs=(VMEM,) * 2,
        compiler_params=params(16),
        name="core_sum",
    )(gq_own, gq_y, got_c)
    got_y = swap(gq_y, 2)
    terms = [terms[0]] + [swap(terms[s], 4 * s) for s in range(1, chunks)]
    vec_out = jax.ShapeDtypeStruct((local_v, dim), F32)
    return pl.pallas_call(
        lambda *refs: finish_kernel(chunks, *refs),
        out_shape=(row_out, vec_out, vec_out),
        in_specs=[VMEM] * (2 + chunks),
        out_specs=(VMEM,) * 3,
        compiler_params=params(16),
        name="finish",
    )(gq_own, got_y, *terms)


def solution(mesh):
    placed = P(("groups", "qry"), None)
    return jax.shard_map(
        body,
        mesh=mesh,
        in_specs=(placed,) * 4,
        out_specs=(placed,) * 3,
        check_vma=False,
    )
```

```python
import math

import jax
import jax.numpy as jnp
from jax import lax
from jax.experimental import pallas as pl
from jax.experimental.pallas import tpu as pltpu
from jax.sharding import PartitionSpec as P

BLK = 256
LOG2E = 1.4426950408889634
LEVELS = 32000.0
TAIL = 16
VMEM = pl.BlockSpec(memory_space=pltpu.VMEM)
HBM = pl.BlockSpec(memory_space=pltpu.HBM)
F32 = jnp.float32
BF16 = jnp.bfloat16
I16 = jnp.int16


def params(mib):
    return pltpu.CompilerParams(vmem_limit_bytes=mib << 20)


def cost(flops, nbytes):
    return pl.CostEstimate(flops=flops, bytes_accessed=nbytes, transcendentals=0)


def encode(x):
    top = jnp.max(jnp.abs(x), axis=0, keepdims=True)
    exponent = jnp.ceil(jnp.log2(jnp.maximum(top, 1e-30)))
    scaled = jnp.round(x * (jnp.exp2(-exponent) * LEVELS))
    return scaled.astype(jnp.int32).astype(I16), exponent


def decode(x, exponent):
    return x.astype(jnp.int32).astype(F32) * (jnp.exp2(exponent) * (1.0 / LEVELS))


def tail_of(exponents):
    rows = jnp.concatenate(exponents, axis=0)
    rest = jnp.zeros((TAIL - rows.shape[0], rows.shape[1]), F32)
    return jnp.concatenate([rows, rest], axis=0).astype(jnp.int32).astype(I16)


def pack_kernel(q_hbm, v_hbm, d_hbm, m_hbm, qm_ref, vd_ref, m_ref, sems):
    rows = q_hbm.shape[0]
    local_v = v_hbm.shape[0]
    copies = [
        pltpu.make_async_copy(m_hbm, m_ref, sems.at[0]),
        pltpu.make_async_copy(v_hbm, vd_ref.at[pl.ds(0, local_v)], sems.at[1]),
        pltpu.make_async_copy(d_hbm, vd_ref.at[pl.ds(local_v, local_v)], sems.at[2]),
        pltpu.make_async_copy(q_hbm, qm_ref.at[pl.ds(0, rows)], sems.at[3]),
    ]
    for copy in copies:
        copy.start()
    copies[0].wait()
    blocks, cols = m_ref.shape
    pad, lanes = qm_ref.shape[0] - rows, qm_ref.shape[1]
    flags = jnp.concatenate([m_ref[...].astype(F32), jnp.zeros((blocks, lanes - cols), F32)], axis=1)
    flags = jnp.concatenate([flags, jnp.zeros((pad - blocks, lanes), F32)], axis=0)
    qm_ref[rows:, :] = flags.astype(BF16)
    for copy in copies[1:]:
        copy.wait()


def tiles(rows, chunks, local_v, scale, qm_refs, vd_refs, gq_refs, gv_ref, w_ref, live_ref):
    me = lax.axis_index("qry")
    wide = 2 * local_v
    group = min(chunks, 4)
    for s in range(chunks):
        w_ref[s * wide : (s + 1) * wide, :] = vd_refs[s][...]
    pad = qm_refs[0].shape[0] - rows
    lanes = lax.broadcasted_iota(jnp.int32, (pad, 128), 1)
    for t, qm_ref in enumerate(qm_refs):
        flags = qm_ref[rows:, :].astype(F32)
        for s in range(chunks):
            col = (jnp.bitwise_xor(me, 4 * s) * local_v) // BLK
            flag = jnp.sum(jnp.where(lanes == col, flags, 0.0), axis=1, keepdims=True)
            live_ref[s, t * pad : (t + 1) * pad, :] = jnp.broadcast_to(
                flag * (-2.0 * scale), (pad, 128)
            )

    def tile(t, r0, height, g):
        q = qm_refs[t][pl.ds(r0, height), :]
        w = w_ref[pl.ds(g * group * wide, group * wide), :]
        both = lax.dot_general(q, w, (((1,), (1,)), ((), ())), preferred_element_type=F32)
        row_blocks = []
        for b in range(height // BLK):
            weights = []
            for c in range(group):
                score = both[b * BLK : (b + 1) * BLK, c * wide : c * wide + local_v]
                error = score - both[b * BLK : (b + 1) * BLK, c * wide + local_v : (c + 1) * wide]
                m = live_ref[g * group + c, pl.ds(t * pad + r0 // BLK + b, 1), :]
                sig = 1.0 / (1.0 + jnp.exp2(score * (-LOG2E)))
                neg = (error * m) * sig
                pos = neg * (error * (0.5 * sig - 0.5) - 1.0)
                weights += [pos.astype(BF16), neg.astype(BF16)]
            row_blocks.append(jnp.concatenate(weights, axis=1))
        weights = jnp.concatenate(row_blocks, axis=0)
        part = jnp.dot(weights, w, preferred_element_type=F32)
        if chunks == group:
            gq_refs[t][pl.ds(r0, height), :] = part
        else:
            gq_refs[t][pl.ds(r0, height), :] = part + jnp.where(
                g == 0, 0.0, gq_refs[t][pl.ds(r0, height), :]
            )
        gv_ref[g] += jnp.dot(q.T, weights, preferred_element_type=F32)

    height = 2 * BLK if rows % (2 * BLK) == 0 else BLK
    for t in range(len(qm_refs)):
        if chunks == group:
            for i in range(rows // height):
                tile(t, i * height, height, 0)
        else:

            def step(n, carry, t=t):
                g = n // (rows // height)
                r0 = pl.multiple_of((n % (rows // height)) * height, height)
                tile(t, r0, height, g)
                return carry

            lax.fori_loop(0, (chunks // group) * (rows // height), step, 0)


def core_sum_kernel(own_ref, got_own_ref, y_ref, got_y_ref, own_out, y_out):
    rows = own_ref.shape[0]
    own_out[...] = own_ref[...] + got_own_ref[...]
    exponents = []
    for r in range(0, rows, BLK):
        code, exponent = encode(y_ref[r : r + BLK, :] + got_y_ref[r : r + BLK, :])
        y_out[r : r + BLK, :] = code
        exponents.append(exponent)
    y_out[rows:, :] = tail_of(exponents)


def finish_kernel(chunks, own_ref, got_ref, term_ref, *refs):
    got_terms, (gq_out, gv_out, gd_out) = refs[: chunks - 1], refs[chunks - 1 :]
    rows = own_ref.shape[0]
    tail = got_ref[rows:, :].astype(jnp.int32).astype(F32)
    for b in range(rows // BLK):
        at = slice(b * BLK, (b + 1) * BLK)
        gq_out[at, :] = own_ref[at, :] + decode(got_ref[at, :], tail[b : b + 1, :])
    total = term_ref[...]
    dim = total.shape[0]
    for got in got_terms:
        tail = got[dim:, :].astype(jnp.int32).astype(F32)
        total = total + decode(got[0:dim, :], tail[0:1, :])
    local_v = gv_out.shape[0]
    gv_out[...] = total[:, :local_v].T
    gd_out[...] = total[:, local_v:].T


def body(queries, vectors, decoded, mask):
    rows, dim = queries.shape
    local_v = vectors.shape[0]
    blocks = mask.shape[0]
    n = lax.axis_size("qry")
    chunks = n // 4
    group = min(chunks, 4)
    wide = 2 * local_v
    scale = 1.0 / math.sqrt(local_v * n)
    pad = -(-blocks // 16) * 16

    def swap(x, bit):
        return lax.ppermute(x, "qry", [(i, i ^ bit) for i in range(n)])

    qm, vd = pl.pallas_call(
        pack_kernel,
        out_shape=(
            jax.ShapeDtypeStruct((rows + pad, dim), BF16),
            jax.ShapeDtypeStruct((wide, dim), BF16),
        ),
        in_specs=[HBM] * 4,
        out_specs=(VMEM, VMEM),
        scratch_shapes=[pltpu.VMEM(mask.shape, mask.dtype), pltpu.SemaphoreType.DMA((4,))],
        compiler_params=params(8),
        name="pack",
    )(queries, vectors, decoded, mask)
    row_out = jax.ShapeDtypeStruct((rows, dim), F32)
    gv_out = jax.ShapeDtypeStruct((chunks // group, dim, group * wide), F32)
    message = jax.ShapeDtypeStruct((dim + TAIL, wide), I16)
    scratch = [
        pltpu.VMEM((chunks * wide, dim), BF16),
        pltpu.VMEM((chunks, 4 * pad, 128), F32),
    ]

    def grads(sets, vds, gv, last, name):
        k = len(sets)

        def kernel(*refs):
            qm_refs, refs = refs[:k], refs[k:]
            vd_refs, refs = refs[:chunks], refs[chunks:]
            gv_in = None
            if gv is not None:
                gv_in, refs = refs[0], refs[1:]
            gq_refs, refs = refs[:k], refs[k:]
            if last:
                outs, (gv_ref, w_ref, live_ref) = refs[:chunks], refs[chunks:]
            else:
                gv_ref, w_ref, live_ref = refs
            gv_ref[...] = jnp.zeros_like(gv_ref) if gv_in is None else gv_in[...]
            tiles(rows, chunks, local_v, scale, qm_refs, vd_refs, gq_refs, gv_ref, w_ref, live_ref)
            if last:
                for s in range(chunks):
                    at = (s % group) * wide
                    term = gv_ref[s // group, :, at : at + wide]
                    if s == 0:
                        outs[0][...] = term
                    else:
                        code, exponent = encode(term)
                        outs[s][0:dim, :] = code
                        outs[s][dim:, :] = tail_of([exponent])

        ends = (
            (jax.ShapeDtypeStruct((dim, wide), F32),) + (message,) * (chunks - 1)
            if last
            else (gv_out,)
        )
        operands = [*sets, *vds] + ([] if gv is None else [gv])
        return pl.pallas_call(
            kernel,
            out_shape=(row_out,) * k + ends,
            in_specs=[VMEM] * len(operands),
            out_specs=(VMEM,) * (k + len(ends)),
            scratch_shapes=([pltpu.VMEM(gv_out.shape, F32)] if last else []) + scratch,
            compiler_params=params(36),
            cost_estimate=cost(12 * k * rows * chunks * wide * dim, 4 << 20),
            name=name,
        )(*operands)

    qm_y = swap(qm, 2)
    qm_c = swap(qm, 1)
    vds = [vd] + [swap(vd, 4 * s) for s in range(1, chunks)]
    qm_y, *vds = lax.optimization_barrier((qm_y, *vds))
    qm_yc = swap(qm_y, 1)
    gq_own, gq_c, gv = grads([qm, qm_c], vds, None, False, "grads_own")
    got_own = swap(gq_c, 1)
    gq_yc, gv = grads([qm_yc], vds, gv, False, "grads_far")
    got_y = swap(gq_yc, 1)
    gq_y, term, *messages = grads([qm_y], vds, gv, True, "grads_y")
    gq_own, gq_message = pl.pallas_call(
        core_sum_kernel,
        out_shape=(row_out, jax.ShapeDtypeStruct((rows + TAIL, dim), I16)),
        in_specs=[VMEM] * 4,
        out_specs=(VMEM,) * 2,
        compiler_params=params(16),
        name="core_sum",
    )(gq_own, got_own, gq_y, got_y)
    got_message = swap(gq_message, 2)
    got_terms = [swap(messages[s - 1], 4 * s) for s in range(1, chunks)]
    vec_out = jax.ShapeDtypeStruct((local_v, dim), F32)
    return pl.pallas_call(
        lambda *refs: finish_kernel(chunks, *refs),
        out_shape=(row_out, vec_out, vec_out),
        in_specs=[VMEM] * (2 + chunks),
        out_specs=(VMEM,) * 3,
        compiler_params=params(16),
        name="finish",
    )(gq_own, got_message, term, *got_terms)


def solution(mesh):
    placed = P(("groups", "qry"), None)
    return jax.shard_map(
        body,
        mesh=mesh,
        in_specs=(placed,) * 4,
        out_specs=(placed,) * 3,
        check_vma=False,
    )
```

```python
import math

import jax
import jax.numpy as jnp
from jax import lax
from jax.experimental import pallas as pl
from jax.experimental.pallas import tpu as pltpu
from jax.sharding import PartitionSpec as P

BLK = 256
LOG2E = 1.4426950408889634
LEVELS = 32000.0
TAIL = 16
VMEM = pl.BlockSpec(memory_space=pltpu.VMEM)
HBM = pl.BlockSpec(memory_space=pltpu.HBM)
F32 = jnp.float32
BF16 = jnp.bfloat16
I16 = jnp.int16


def params(mib):
    return pltpu.CompilerParams(vmem_limit_bytes=mib << 20)


def cost(flops, nbytes):
    return pl.CostEstimate(flops=flops, bytes_accessed=nbytes, transcendentals=0)


def encode(x):
    top = jnp.max(jnp.abs(x), axis=0, keepdims=True)
    exponent = jnp.ceil(jnp.log2(jnp.maximum(top, 1e-30)))
    scaled = jnp.round(x * (jnp.exp2(-exponent) * LEVELS))
    return scaled.astype(jnp.int32).astype(I16), exponent


def decode(x, exponent):
    return x.astype(jnp.int32).astype(F32) * (jnp.exp2(exponent) * (1.0 / LEVELS))


def tail_of(exponents):
    rows = jnp.concatenate(exponents, axis=0)
    rest = jnp.zeros((TAIL - rows.shape[0], rows.shape[1]), F32)
    return jnp.concatenate([rows, rest], axis=0).astype(jnp.int32).astype(I16)


def pack_kernel(q_hbm, v_hbm, d_hbm, m_hbm, qm_ref, vd_ref, m_ref, sems):
    rows = q_hbm.shape[0]
    local_v = v_hbm.shape[0]
    copies = [
        pltpu.make_async_copy(m_hbm, m_ref, sems.at[0]),
        pltpu.make_async_copy(v_hbm, vd_ref.at[pl.ds(0, local_v)], sems.at[1]),
        pltpu.make_async_copy(d_hbm, vd_ref.at[pl.ds(local_v, local_v)], sems.at[2]),
        pltpu.make_async_copy(q_hbm, qm_ref.at[pl.ds(0, rows)], sems.at[3]),
    ]
    for copy in copies:
        copy.start()
    copies[0].wait()
    blocks, cols = m_ref.shape
    pad, lanes = qm_ref.shape[0] - rows, qm_ref.shape[1]
    flags = jnp.concatenate([m_ref[...].astype(F32), jnp.zeros((blocks, lanes - cols), F32)], axis=1)
    flags = jnp.concatenate([flags, jnp.zeros((pad - blocks, lanes), F32)], axis=0)
    qm_ref[rows:, :] = flags.astype(BF16)
    for copy in copies[1:]:
        copy.wait()


def tile_grads(q, w, live, chunks, local_v):
    wide = 2 * local_v
    both = lax.dot_general(q, w, (((1,), (1,)), ((), ())), preferred_element_type=F32)
    row_blocks = []
    for b in range(q.shape[0] // BLK):
        weights = []
        for c in range(chunks):
            score = both[b * BLK : (b + 1) * BLK, c * wide : c * wide + local_v]
            error = score - both[b * BLK : (b + 1) * BLK, c * wide + local_v : (c + 1) * wide]
            sig = 1.0 / (1.0 + jnp.exp2(score * (-LOG2E)))
            neg = (error * live(b, c)) * sig
            pos = neg * (error * (0.5 * sig - 0.5) - 1.0)
            weights += [pos.astype(BF16), neg.astype(BF16)]
        row_blocks.append(jnp.concatenate(weights, axis=1))
    weights = jnp.concatenate(row_blocks, axis=0)
    return (
        jnp.dot(weights, w, preferred_element_type=F32),
        jnp.dot(q.T, weights, preferred_element_type=F32),
    )


def grads(sets, vds, group, rows, local_v, scale, gqs, gvs, send, code_last, name):
    k, m = len(sets), len(vds)
    dim = sets[0].shape[1]
    pad = sets[0].shape[0] - rows
    wide = 2 * local_v
    part = min(m, 4)
    height = 2 * BLK if rows % (2 * BLK) == 0 else BLK

    def kernel(*refs):
        qm_refs, refs = refs[:k], refs[k:]
        vd_refs, refs = refs[:m], refs[m:]
        gq_ins, gv_ins = None, None
        if gqs is not None:
            gq_ins, refs = refs[:k], refs[k:]
        if gvs is not None:
            gv_ins, refs = refs[:m], refs[m:]
        gq_refs, refs = refs[:k], refs[k:]
        gv_outs, (gv_ref, w_ref, live_ref) = refs[:m], refs[m:]
        me = lax.axis_index("qry")
        lanes = lax.broadcasted_iota(jnp.int32, (pad, 128), 1)
        for s in range(m):
            w_ref[s * wide : (s + 1) * wide, :] = vd_refs[s][...]
            gv_ref[:, s * wide : (s + 1) * wide] = (
                jnp.zeros((dim, wide), F32) if gv_ins is None else gv_ins[s][...]
            )
        for t in range(k):
            flags = qm_refs[t][rows:, :].astype(F32)
            for s in range(m):
                col = (jnp.bitwise_xor(me, 4 * group[s]) * local_v) // BLK
                flag = jnp.sum(jnp.where(lanes == col, flags, 0.0), axis=1, keepdims=True)
                live_ref[s, t * pad : (t + 1) * pad, :] = jnp.broadcast_to(
                    flag * (-2.0 * scale), (pad, 128)
                )

        exponents = []

        def tile(t, r0, first):
            def live(b, c):
                return live_ref[first + c, pl.ds(t * pad + r0 // BLK + b, 1), :]

            at = slice(first * wide, (first + part) * wide)
            q = qm_refs[t][pl.ds(r0, height), :]
            gq, gv = tile_grads(q, w_ref[at, :], live, part, local_v)
            if first > 0:
                gq = gq + gq_refs[t][pl.ds(r0, height), :]
            elif gq_ins is not None:
                gq = gq + gq_ins[t][pl.ds(r0, height), :]
            if code_last and t == k - 1:
                for b in range(0, height, BLK):
                    code, exponent = encode(gq[b : b + BLK])
                    gq_refs[t][r0 + b : r0 + b + BLK, :] = code
                    exponents.append(exponent)
            else:
                gq_refs[t][pl.ds(r0, height), :] = gq
            gv_ref[:, at] += gv

        for t in range(k):
            for first in range(0, m, part):
                if m <= 4:
                    for i in range(rows // height):
                        tile(t, i * height, first)
                else:

                    def step(i, carry, t=t, first=first):
                        tile(t, pl.multiple_of(i * height, height), first)
                        return carry

                    lax.fori_loop(0, rows // height, step, 0)
        if code_last:
            gq_refs[k - 1][rows:, :] = tail_of(exponents)
        for s in range(m):
            term = gv_ref[:, s * wide : (s + 1) * wide]
            if group[s] in send:
                code, exponent = encode(term)
                gv_outs[s][0:dim, :] = code
                gv_outs[s][dim:, :] = tail_of([exponent])
            else:
                gv_outs[s][...] = term

    operands = [*sets, *vds, *(gqs or []), *(gvs or [])]
    outs = [jax.ShapeDtypeStruct((rows, dim), F32)] * k + [
        jax.ShapeDtypeStruct((dim + TAIL, wide), I16)
        if s in send
        else jax.ShapeDtypeStruct((dim, wide), F32)
        for s in group
    ]
    if code_last:
        outs[k - 1] = jax.ShapeDtypeStruct((rows + TAIL, dim), I16)
    res = pl.pallas_call(
        kernel,
        out_shape=tuple(outs),
        in_specs=[VMEM] * len(operands),
        out_specs=(VMEM,) * len(outs),
        scratch_shapes=[
            pltpu.VMEM((dim, m * wide), F32),
            pltpu.VMEM((m * wide, dim), BF16),
            pltpu.VMEM((m, k * pad, 128), F32),
        ],
        compiler_params=params(32),
        cost_estimate=cost(k * rows * m * wide, 1 << 10),
        name=name,
    )(*operands)
    return list(res[:k]), list(res[k:])


def core_sum_kernel(y_ref, got_y_ref, y_out):
    rows = y_ref.shape[0]
    exponents = []
    for r in range(0, rows, BLK):
        code, exponent = encode(y_ref[r : r + BLK, :] + got_y_ref[r : r + BLK, :])
        y_out[r : r + BLK, :] = code
        exponents.append(exponent)
    y_out[rows : rows + TAIL, :] = tail_of(exponents)
    y_out[rows + TAIL :, :] = jnp.zeros((y_out.shape[0] - rows - TAIL, y_out.shape[1]), I16)


def finish_kernel(chunks, own_ref, got_own_ref, got_ref, term_ref, *refs):
    got_terms, (gq_out, gv_out, gd_out) = refs[: chunks - 1], refs[chunks - 1 :]
    rows = own_ref.shape[0]
    tail = got_ref[rows:, :].astype(jnp.int32).astype(F32)
    own_tail = got_own_ref[rows:, :].astype(jnp.int32).astype(F32)
    for b in range(rows // BLK):
        at = slice(b * BLK, (b + 1) * BLK)
        own = own_ref[at, :] + decode(got_own_ref[at, :], own_tail[b : b + 1, :])
        gq_out[at, :] = own + decode(got_ref[at, :], tail[b : b + 1, :])
    total = term_ref[...]
    dim = total.shape[0]
    for got in got_terms:
        tail = got[dim:, :].astype(jnp.int32).astype(F32)
        total = total + decode(got[0:dim, :], tail[0:1, :])
    local_v = gv_out.shape[0]
    gv_out[...] = total[:, :local_v].T
    gd_out[...] = total[:, local_v:].T


def body(queries, vectors, decoded, mask):
    rows, dim = queries.shape
    local_v = vectors.shape[0]
    blocks = mask.shape[0]
    n = lax.axis_size("qry")
    chunks = n // 4
    wide = 2 * local_v
    scale = 1.0 / math.sqrt(local_v * n)
    pad = -(-blocks // 16) * 16

    def swap(x, bit):
        return lax.ppermute(x, "qry", [(i, i ^ bit) for i in range(n)])

    qm, vd = pl.pallas_call(
        pack_kernel,
        out_shape=(
            jax.ShapeDtypeStruct((rows + pad, dim), BF16),
            jax.ShapeDtypeStruct((wide, dim), BF16),
        ),
        in_specs=[HBM] * 4,
        out_specs=(VMEM, VMEM),
        scratch_shapes=[pltpu.VMEM(mask.shape, mask.dtype), pltpu.SemaphoreType.DMA((4,))],
        compiler_params=params(60),
        name="pack",
    )(queries, vectors, decoded, mask)
    row_out = jax.ShapeDtypeStruct((rows, dim), F32)
    quarter = chunks // 4
    groups = [tuple(range(g * quarter, (g + 1) * quarter)) for g in range(4)]
    done = {"yc": groups[0] + groups[1], "own_3": groups[3], "own_2": groups[2]}

    def add(sets, which, gqs, gvs, name):
        group = sum((groups[g] for g in which), ())
        ready = [s for s in group if s > 0 and s in done.get(name, ())]
        return grads(
            sets, [vds[s] for s in group], group, rows, local_v, scale, gqs, gvs, ready,
            name == "own_2", name,
        )

    qm_y = swap(qm, 2)
    qm_c = swap(qm, 1)
    vds = [vd] + [swap(vd, 4 * s) for s in range(1, chunks)]
    own, half = [qm, qm_c], 2 * quarter
    gq_o, gv0 = add(own, [0], None, None, "own_0")
    gq_o, gv1 = add(own, [1], gq_o, None, "own_1")
    gq_y, gv01 = add([qm_y], [0, 1], None, gv0 + gv1, "y_01")
    qm_y, gq_y, gv01, vds[half:] = lax.optimization_barrier((qm_y, gq_y, gv01, vds[half:]))
    qm_yc = swap(qm_y, 1)
    gq_y, gv23 = add([qm_y], [2, 3], gq_y, None, "y_23")
    gq_yc, gvs = add([qm_yc], [0, 1, 2, 3], None, gv01 + gv23, "yc")
    got_y = swap(gq_yc[0], 1)
    gq_o, gv3 = add(own, [3], gq_o, gvs[half + quarter :], "own_3")
    gq_message = pl.pallas_call(
        core_sum_kernel,
        out_shape=jax.ShapeDtypeStruct((rows + 2 * TAIL, dim), I16),
        in_specs=[VMEM] * 2,
        out_specs=VMEM,
        compiler_params=params(16),
        name="core_sum",
    )(gq_y[0], got_y)
    gq_o, gq_message = lax.optimization_barrier((gq_o, gq_message))
    gq_o, gv2 = add(own, [2], gq_o, gvs[half : half + quarter], "own_2")
    gq_own, gq_c = gq_o
    got_own = swap(gq_c, 1)
    term, *near = gvs[:half]
    near = [swap(x, 4 * s) for s, x in enumerate(near, 1)]
    got_terms = near + [swap(x, 4 * s) for s, x in enumerate(gv2 + gv3, half)]
    got_message = swap(gq_message, 2)
    vec_out = jax.ShapeDtypeStruct((local_v, dim), F32)
    return pl.pallas_call(
        lambda *refs: finish_kernel(chunks, *refs),
        out_shape=(row_out, vec_out, vec_out),
        in_specs=[VMEM] * (3 + chunks),
        out_specs=(VMEM,) * 3,
        compiler_params=params(16),
        name="finish",
    )(gq_own, got_own, got_message, term, *got_terms)


def solution(mesh):
    placed = P(("groups", "qry"), None)
    return jax.shard_map(
        body,
        mesh=mesh,
        in_specs=(placed,) * 4,
        out_specs=(placed,) * 3,
        check_vma=False,
    )
```

```python
import math

import jax
import jax.numpy as jnp
from jax import lax
from jax.experimental import pallas as pl
from jax.experimental.pallas import tpu as pltpu
from jax.sharding import PartitionSpec as P

BLK = 256
LOG2E = 1.4426950408889634
LEVELS = 32000.0
TAIL = 16
VMEM = pl.BlockSpec(memory_space=pltpu.VMEM)
HBM = pl.BlockSpec(memory_space=pltpu.HBM)
F32 = jnp.float32
BF16 = jnp.bfloat16
I16 = jnp.int16


def params(mib):
    return pltpu.CompilerParams(vmem_limit_bytes=mib << 20)


def cost(flops, nbytes):
    return pl.CostEstimate(flops=flops, bytes_accessed=nbytes, transcendentals=0)


def encode(x):
    top = jnp.max(jnp.abs(x), axis=0, keepdims=True)
    exponent = jnp.ceil(jnp.log2(jnp.maximum(top, 1e-30)))
    scaled = jnp.round(x * (jnp.exp2(-exponent) * LEVELS))
    return scaled.astype(jnp.int32).astype(I16), exponent


def decode(x, exponent):
    return x.astype(jnp.int32).astype(F32) * (jnp.exp2(exponent) * (1.0 / LEVELS))


def tail_of(exponents):
    rows = jnp.concatenate(exponents, axis=0)
    rest = jnp.zeros((TAIL - rows.shape[0], rows.shape[1]), F32)
    return jnp.concatenate([rows, rest], axis=0).astype(jnp.int32).astype(I16)


def encode_rows(x_ref, out_ref):
    rows = x_ref.shape[0]
    exponents = []
    for r in range(0, rows, BLK):
        code, exponent = encode(x_ref[r : r + BLK, :])
        out_ref[r : r + BLK, :] = code
        exponents.append(exponent)
    out_ref[rows : rows + TAIL, :] = tail_of(exponents)
    if out_ref.shape[0] > rows + TAIL:
        rest = (out_ref.shape[0] - rows - TAIL, out_ref.shape[1])
        out_ref[rows + TAIL :, :] = jnp.zeros(rest, I16)


def pack_kernel(q_hbm, v_hbm, d_hbm, m_hbm, qm_ref, vd_ref, m_ref, sems):
    rows = q_hbm.shape[0]
    local_v = v_hbm.shape[0]
    copies = [
        pltpu.make_async_copy(m_hbm, m_ref, sems.at[0]),
        pltpu.make_async_copy(v_hbm, vd_ref.at[pl.ds(0, local_v)], sems.at[1]),
        pltpu.make_async_copy(d_hbm, vd_ref.at[pl.ds(local_v, local_v)], sems.at[2]),
        pltpu.make_async_copy(q_hbm, qm_ref.at[pl.ds(0, rows)], sems.at[3]),
    ]
    for copy in copies:
        copy.start()
    copies[0].wait()
    blocks, cols = m_ref.shape
    pad, lanes = qm_ref.shape[0] - rows, qm_ref.shape[1]
    flags = jnp.concatenate([m_ref[...].astype(F32), jnp.zeros((blocks, lanes - cols), F32)], axis=1)
    flags = jnp.concatenate([flags, jnp.zeros((pad - blocks, lanes), F32)], axis=0)
    qm_ref[rows:, :] = flags.astype(BF16)
    for copy in copies[1:]:
        copy.wait()


def live_table(flags, chunks, local_v, scale):
    me = lax.axis_index("qry")
    lanes = flags.shape[1]
    rows = lax.broadcasted_iota(jnp.int32, (lanes, 128), 0)
    cols = [(jnp.bitwise_xor(me, 4 * s) * local_v) // BLK for s in range(chunks)]
    onehot = jnp.concatenate([(rows == col).astype(F32) for col in cols], axis=1)
    return jnp.dot(flags, onehot.astype(BF16), preferred_element_type=F32) * (-2.0 * scale)


def tile_weights(q, w, live, chunks, local_v):
    wide = 2 * local_v
    both = lax.dot_general(q, w, (((1,), (1,)), ((), ())), preferred_element_type=F32)
    row_blocks = []
    for b in range(q.shape[0] // BLK):
        weights = []
        for c in range(chunks):
            score = both[b * BLK : (b + 1) * BLK, c * wide : c * wide + local_v]
            error = score - both[b * BLK : (b + 1) * BLK, c * wide + local_v : (c + 1) * wide]
            sig = 1.0 / (1.0 + jnp.exp2(score * (-LOG2E)))
            neg = (error * live(b, c)) * sig
            pos = neg * (error * (0.5 * sig - 0.5) - 1.0)
            weights += [pos.astype(BF16), neg.astype(BF16)]
        row_blocks.append(jnp.concatenate(weights, axis=1))
    return jnp.concatenate(row_blocks, axis=0)


def grads(sets, vds, group, chunks, rows, local_v, scale, table, gqs, gvs, send, code_last, name):
    k, m = len(sets), len(vds)
    dim = sets[0].shape[1]
    pad = sets[0].shape[0] - rows
    wide = 2 * local_v
    part = min(m, 4)
    height = 2 * BLK if rows % (2 * BLK) == 0 else BLK
    fresh = table is None

    def kernel(*refs):
        qm_refs, refs = refs[:k], refs[k:]
        vd_refs, refs = refs[:m], refs[m:]
        gq_ins, gv_ins = None, None
        if not fresh:
            table_ref, refs = refs[0], refs[1:]
        if gqs is not None:
            gq_ins, refs = refs[:k], refs[k:]
        if gvs is not None:
            gv_ins, refs = refs[:m], refs[m:]
        gq_refs, refs = refs[:k], refs[k:]
        gv_outs, refs = refs[:m], refs[m:]
        if fresh:
            table_ref, refs = refs[0], refs[1:]
            for t in range(k):
                table = live_table(qm_refs[t][rows:, :], chunks, local_v, scale)
                for s in range(chunks):
                    table_ref[s, t * pad : (t + 1) * pad, :] = table[:, s * 128 : (s + 1) * 128]
        gv_ref, w_ref, last_ref = refs
        for s in range(m):
            w_ref[s * wide : (s + 1) * wide, :] = vd_refs[s][...]
            gv_ref[:, s * wide : (s + 1) * wide] = (
                jnp.zeros((dim, wide), F32) if gv_ins is None else gv_ins[s][...]
            )
        outs = [*gq_refs[: k - 1], last_ref if code_last else gq_refs[k - 1]]

        def tile(t, r0, first):
            def live(b, c):
                s = group[first + c]
                return table_ref[s, pl.ds(t * pad + r0 // BLK + b, 1), :]

            w = w_ref[first * wide : (first + part) * wide, :]
            weights = tile_weights(qm_refs[t][pl.ds(r0, height), :], w, live, part, local_v)
            gq = jnp.dot(weights, w, preferred_element_type=F32)
            if first > 0:
                gq = gq + outs[t][pl.ds(r0, height), :]
            elif gq_ins is not None:
                gq = gq + gq_ins[t][pl.ds(r0, height), :]
            outs[t][pl.ds(r0, height), :] = gq
            return weights

        if m <= 4:
            weights = [tile(t, r0, 0) for t in range(k) for r0 in range(0, rows, height)]
            q = jnp.concatenate([ref[0:rows, :] for ref in qm_refs], axis=0)
            gv_ref[...] += jnp.dot(
                q.T, jnp.concatenate(weights, axis=0), preferred_element_type=F32
            )
        else:
            for t in range(k):
                for first in range(0, m, part):

                    def step(i, carry, t=t, first=first):
                        r0 = pl.multiple_of(i * height, height)
                        weights = tile(t, r0, first)
                        q = qm_refs[t][pl.ds(r0, height), :]
                        gv_ref[:, first * wide : (first + part) * wide] += jnp.dot(
                            q.T, weights, preferred_element_type=F32
                        )
                        return carry

                    lax.fori_loop(0, rows // height, step, 0)
        if code_last:
            encode_rows(last_ref, gq_refs[k - 1])
        for s in range(m):
            term = gv_ref[:, s * wide : (s + 1) * wide]
            if group[s] in send:
                code, exponent = encode(term)
                gv_outs[s][0:dim, :] = code
                gv_outs[s][dim:, :] = tail_of([exponent])
            else:
                gv_outs[s][...] = term

    operands = [*sets, *vds, *([] if fresh else [table]), *(gqs or []), *(gvs or [])]
    outs = [jax.ShapeDtypeStruct((rows, dim), F32)] * k + [
        jax.ShapeDtypeStruct((dim + TAIL, wide), I16)
        if s in send
        else jax.ShapeDtypeStruct((dim, wide), F32)
        for s in group
    ]
    if code_last:
        outs[k - 1] = jax.ShapeDtypeStruct((rows + TAIL, dim), I16)
    if fresh:
        outs.append(jax.ShapeDtypeStruct((chunks, k * pad, 128), F32))
    res = pl.pallas_call(
        kernel,
        out_shape=tuple(outs),
        in_specs=[VMEM] * len(operands),
        out_specs=(VMEM,) * len(outs),
        scratch_shapes=[
            pltpu.VMEM((dim, m * wide), F32),
            pltpu.VMEM((m * wide, dim), BF16),
            pltpu.VMEM((rows if code_last else 8, dim), F32),
        ],
        compiler_params=params(32),
        cost_estimate=cost(k * rows * m * wide, 1 << 10),
        name=name,
    )(*operands)
    return list(res[:k]), list(res[k : k + m]), res[-1] if fresh else table


def core_sum_kernel(y_ref, got_y_ref, y_out, sum_ref):
    sum_ref[...] = y_ref[...] + got_y_ref[...]
    encode_rows(sum_ref, y_out)


def finish_q_kernel(own_ref, got_own_ref, got_ref, gq_out):
    rows = own_ref.shape[0]
    tail = got_ref[rows : rows + TAIL, :].astype(jnp.int32).astype(F32)
    own_tail = got_own_ref[rows:, :].astype(jnp.int32).astype(F32)
    for b in range(rows // BLK):
        at = slice(b * BLK, (b + 1) * BLK)
        own = own_ref[at, :] + decode(got_own_ref[at, :], own_tail[b : b + 1, :])
        gq_out[at, :] = own + decode(got_ref[at, :], tail[b : b + 1, :])


def finish_v_kernel(term_ref, *refs):
    got_terms, (gv_out, gd_out) = refs[:-2], refs[-2:]
    total = term_ref[...]
    dim = total.shape[0]
    for got in got_terms:
        tail = got[dim:, :].astype(jnp.int32).astype(F32)
        total = total + decode(got[0:dim, :], tail[0:1, :])
    local_v = gv_out.shape[0]
    gv_out[...] = total[:, :local_v].T
    gd_out[...] = total[:, local_v:].T


def body(queries, vectors, decoded, mask):
    rows, dim = queries.shape
    local_v = vectors.shape[0]
    blocks = mask.shape[0]
    n = lax.axis_size("qry")
    chunks = n // 4
    wide = 2 * local_v
    scale = 1.0 / math.sqrt(local_v * n)
    pad = -(-blocks // 16) * 16

    def swap(x, bit):
        return lax.ppermute(x, "qry", [(i, i ^ bit) for i in range(n)])

    qm, vd = pl.pallas_call(
        pack_kernel,
        out_shape=(
            jax.ShapeDtypeStruct((rows + pad, dim), BF16),
            jax.ShapeDtypeStruct((wide, dim), BF16),
        ),
        in_specs=[HBM] * 4,
        out_specs=(VMEM, VMEM),
        scratch_shapes=[pltpu.VMEM(mask.shape, mask.dtype), pltpu.SemaphoreType.DMA((4,))],
        compiler_params=params(8),
        name="pack",
    )(*[pltpu.with_memory_space_constraint(x, pltpu.HBM) for x in (queries, vectors, decoded, mask)])
    row_out = jax.ShapeDtypeStruct((rows, dim), F32)
    quarter = chunks // 4
    groups = [tuple(range(g * quarter, (g + 1) * quarter)) for g in range(4)]
    half = 2 * quarter

    def add(sets, which, table, gqs, gvs, send, code_last, name):
        group = sum((groups[g] for g in which), ())
        return grads(
            sets, [vds[s] for s in group], group, chunks, rows, local_v, scale,
            table, gqs, gvs, send, code_last, name,
        )

    qm_y = swap(qm, 2)
    qm_c = swap(qm, 1)
    vds = [vd] + [swap(vd, 4 * s) for s in range(1, chunks)]
    own = [qm, qm_c]
    gq_o, gv0, table = add(own, [0], None, None, None, (), False, "own_0")
    gq_o, gv1, _ = add(own, [1], table, gq_o, None, (), False, "own_1")
    gq_y, gv01, table_y = add([qm_y], [0, 1], None, None, gv0 + gv1, (), False, "y_01")
    qm_y, gq_y, gv01, vds[half:] = lax.optimization_barrier((qm_y, gq_y, gv01, vds[half:]))
    qm_yc = swap(qm_y, 1)
    gq_y, gv23, _ = add([qm_y], [2, 3], table_y, gq_y, None, (), False, "y_23")
    near = tuple(range(1, half))
    gq_yc, gvs, _ = add([qm_yc], [0, 1, 2, 3], None, None, gv01 + gv23, near, False, "yc")
    got_y = swap(gq_yc[0], 1)
    far = tuple(range(half, chunks))
    gq_o, gv23, _ = add(own, [2, 3], table, gq_o, gvs[half:], far, True, "own_23")
    got_y, gv23 = lax.optimization_barrier((got_y, gv23))
    gq_message = pl.pallas_call(
        core_sum_kernel,
        out_shape=jax.ShapeDtypeStruct((rows + 2 * TAIL, dim), I16),
        in_specs=[VMEM] * 2,
        out_specs=VMEM,
        scratch_shapes=[pltpu.VMEM((rows, dim), F32)],
        compiler_params=params(16),
        name="core_sum",
    )(gq_y[0], got_y)
    gq_own, gq_c = gq_o
    got_own = swap(gq_c, 1)
    term, *messages = gvs[:half] + gv23
    got_message = swap(gq_message, 2)
    got_terms = [swap(x, 4 * s) for s, x in enumerate(messages, 1)]
    grad_q = pl.pallas_call(
        finish_q_kernel,
        out_shape=row_out,
        in_specs=[VMEM] * 3,
        out_specs=VMEM,
        compiler_params=params(16),
        name="finish_q",
    )(gq_own, got_own, got_message)
    grad_q, term = lax.optimization_barrier((grad_q, term))
    vec_out = jax.ShapeDtypeStruct((local_v, dim), F32)
    grad_v, grad_d = pl.pallas_call(
        finish_v_kernel,
        out_shape=(vec_out, vec_out),
        in_specs=[VMEM] * chunks,
        out_specs=(VMEM,) * 2,
        compiler_params=params(16),
        name="finish_v",
    )(term, *got_terms)
    return grad_q, grad_v, grad_d


def solution(mesh):
    placed = P(("groups", "qry"), None)
    return jax.shard_map(
        body,
        mesh=mesh,
        in_specs=(placed,) * 4,
        out_specs=(placed,) * 3,
        check_vma=False,
    )
```

```python
import math

import jax
import jax.numpy as jnp
from jax import lax
from jax.experimental import pallas as pl
from jax.experimental.pallas import tpu as pltpu
from jax.sharding import PartitionSpec as P

BLK = 256
LOG2E = 1.4426950408889634
LEVELS = 32000.0
TAIL = 16
VMEM = pl.BlockSpec(memory_space=pltpu.VMEM)
HBM = pl.BlockSpec(memory_space=pltpu.HBM)
F32 = jnp.float32
BF16 = jnp.bfloat16
I16 = jnp.int16


def params(mib):
    return pltpu.CompilerParams(vmem_limit_bytes=mib << 20)


def cost(flops, nbytes):
    return pl.CostEstimate(flops=flops, bytes_accessed=nbytes, transcendentals=0)


def encode(x):
    top = jnp.max(jnp.abs(x), axis=0, keepdims=True)
    exponent = jnp.ceil(jnp.log2(jnp.maximum(top, 1e-30)))
    scaled = jnp.round(x * (jnp.exp2(-exponent) * LEVELS))
    return scaled.astype(jnp.int32).astype(I16), exponent


def decode(x, exponent):
    return x.astype(jnp.int32).astype(F32) * (jnp.exp2(exponent) * (1.0 / LEVELS))


def tail_of(exponents):
    rows = jnp.concatenate(exponents, axis=0)
    rest = jnp.zeros((TAIL - rows.shape[0], rows.shape[1]), F32)
    return jnp.concatenate([rows, rest], axis=0).astype(jnp.int32).astype(I16)


def encode_rows(x_ref, out_ref):
    rows = x_ref.shape[0]
    exponents = []
    for r in range(0, rows, BLK):
        code, exponent = encode(x_ref[r : r + BLK, :])
        out_ref[r : r + BLK, :] = code
        exponents.append(exponent)
    out_ref[rows : rows + TAIL, :] = tail_of(exponents)
    if out_ref.shape[0] > rows + TAIL:
        rest = (out_ref.shape[0] - rows - TAIL, out_ref.shape[1])
        out_ref[rows + TAIL :, :] = jnp.zeros(rest, I16)


def pack_kernel(q_hbm, v_hbm, d_hbm, m_hbm, qm_ref, vd_ref, m_ref, sems):
    rows = q_hbm.shape[0]
    local_v = v_hbm.shape[0]
    copies = [
        pltpu.make_async_copy(m_hbm, m_ref, sems.at[0]),
        pltpu.make_async_copy(v_hbm, vd_ref.at[pl.ds(0, local_v)], sems.at[1]),
        pltpu.make_async_copy(d_hbm, vd_ref.at[pl.ds(local_v, local_v)], sems.at[2]),
        pltpu.make_async_copy(q_hbm, qm_ref.at[pl.ds(0, rows)], sems.at[3]),
    ]
    for copy in copies:
        copy.start()
    copies[0].wait()
    blocks, cols = m_ref.shape
    pad, lanes = qm_ref.shape[0] - rows, qm_ref.shape[1]
    flags = jnp.concatenate([m_ref[...].astype(F32), jnp.zeros((blocks, lanes - cols), F32)], axis=1)
    flags = jnp.concatenate([flags, jnp.zeros((pad - blocks, lanes), F32)], axis=0)
    qm_ref[rows:, :] = flags.astype(BF16)
    for copy in copies[1:]:
        copy.wait()


def live_table(flags, chunks, local_v, scale):
    me = lax.axis_index("qry")
    lanes = flags.shape[1]
    rows = lax.broadcasted_iota(jnp.int32, (lanes, 128), 0)
    cols = [(jnp.bitwise_xor(me, 4 * s) * local_v) // BLK for s in range(chunks)]
    onehot = jnp.concatenate([(rows == col).astype(F32) for col in cols], axis=1)
    return jnp.dot(flags, onehot.astype(BF16), preferred_element_type=F32) * (-2.0 * scale)


def tile_weights(q, w, live, chunks, local_v):
    wide = 2 * local_v
    both = lax.dot_general(q, w, (((1,), (1,)), ((), ())), preferred_element_type=F32)
    row_blocks = []
    for b in range(q.shape[0] // BLK):
        weights = []
        for c in range(chunks):
            score = both[b * BLK : (b + 1) * BLK, c * wide : c * wide + local_v]
            error = score - both[b * BLK : (b + 1) * BLK, c * wide + local_v : (c + 1) * wide]
            sig = 1.0 / (1.0 + jnp.exp2(score * (-LOG2E)))
            neg = (error * live(b, c)) * sig
            pos = neg * (error * (0.5 * sig - 0.5) - 1.0)
            weights += [pos.astype(BF16), neg.astype(BF16)]
        row_blocks.append(jnp.concatenate(weights, axis=1))
    return jnp.concatenate(row_blocks, axis=0)


def grads(sets, vds, group, chunks, rows, local_v, scale, table, gqs, gvs, send, code_last, name):
    k, m = len(sets), len(vds)
    dim = sets[0].shape[1]
    pad = sets[0].shape[0] - rows
    wide = 2 * local_v
    part = min(m, 4)
    height = 2 * BLK if rows % (2 * BLK) == 0 else BLK
    fresh = table is None

    def kernel(*refs):
        qm_refs, refs = refs[:k], refs[k:]
        vd_refs, refs = refs[:m], refs[m:]
        gq_ins, gv_ins = None, None
        if not fresh:
            table_ref, refs = refs[0], refs[1:]
        if gqs is not None:
            gq_ins, refs = refs[:k], refs[k:]
        if gvs is not None:
            gv_ins, refs = refs[:m], refs[m:]
        gq_refs, refs = refs[:k], refs[k:]
        gv_outs, refs = refs[:m], refs[m:]
        if fresh:
            table_ref, refs = refs[0], refs[1:]
            for t in range(k):
                table = live_table(qm_refs[t][rows:, :], chunks, local_v, scale)
                for s in range(chunks):
                    table_ref[s, t * pad : (t + 1) * pad, :] = table[:, s * 128 : (s + 1) * 128]
        gv_ref, w_ref, last_ref = refs
        for s in range(m):
            w_ref[s * wide : (s + 1) * wide, :] = vd_refs[s][...]
            gv_ref[:, s * wide : (s + 1) * wide] = (
                jnp.zeros((dim, wide), F32) if gv_ins is None else gv_ins[s][...]
            )
        outs = [*gq_refs[: k - 1], last_ref if code_last else gq_refs[k - 1]]

        def tile(t, r0, first):
            def live(b, c):
                s = group[first + c]
                return table_ref[s, pl.ds(t * pad + r0 // BLK + b, 1), :]

            w = w_ref[first * wide : (first + part) * wide, :]
            weights = tile_weights(qm_refs[t][pl.ds(r0, height), :], w, live, part, local_v)
            gq = jnp.dot(weights, w, preferred_element_type=F32)
            if first > 0:
                gq = gq + outs[t][pl.ds(r0, height), :]
            elif gq_ins is not None:
                gq = gq + gq_ins[t][pl.ds(r0, height), :]
            outs[t][pl.ds(r0, height), :] = gq
            return weights

        if m <= 4:
            weights = [tile(t, r0, 0) for t in range(k) for r0 in range(0, rows, height)]
            q = jnp.concatenate([ref[0:rows, :] for ref in qm_refs], axis=0)
            gv_ref[...] += jnp.dot(
                q.T, jnp.concatenate(weights, axis=0), preferred_element_type=F32
            )
        else:
            for t in range(k):
                for first in range(0, m, part):

                    def step(i, carry, t=t, first=first):
                        r0 = pl.multiple_of(i * height, height)
                        weights = tile(t, r0, first)
                        q = qm_refs[t][pl.ds(r0, height), :]
                        gv_ref[:, first * wide : (first + part) * wide] += jnp.dot(
                            q.T, weights, preferred_element_type=F32
                        )
                        return carry

                    lax.fori_loop(0, rows // height, step, 0)
        if code_last:
            encode_rows(last_ref, gq_refs[k - 1])
        for s in range(m):
            term = gv_ref[:, s * wide : (s + 1) * wide]
            if group[s] in send:
                code, exponent = encode(term)
                gv_outs[s][0:dim, :] = code
                gv_outs[s][dim:, :] = tail_of([exponent])
            else:
                gv_outs[s][...] = term

    operands = [*sets, *vds, *([] if fresh else [table]), *(gqs or []), *(gvs or [])]
    outs = [jax.ShapeDtypeStruct((rows, dim), F32)] * k + [
        jax.ShapeDtypeStruct((dim + TAIL, wide), I16)
        if s in send
        else jax.ShapeDtypeStruct((dim, wide), F32)
        for s in group
    ]
    if code_last:
        outs[k - 1] = jax.ShapeDtypeStruct((rows + TAIL, dim), I16)
    if fresh:
        outs.append(jax.ShapeDtypeStruct((chunks, k * pad, 128), F32))
    res = pl.pallas_call(
        kernel,
        out_shape=tuple(outs),
        in_specs=[VMEM] * len(operands),
        out_specs=(VMEM,) * len(outs),
        scratch_shapes=[
            pltpu.VMEM((dim, m * wide), F32),
            pltpu.VMEM((m * wide, dim), BF16),
            pltpu.VMEM((rows if code_last else 8, dim), F32),
        ],
        compiler_params=params(32),
        cost_estimate=cost(k * rows * m * wide, 1 << 10),
        name=name,
    )(*operands)
    return list(res[:k]), list(res[k : k + m]), res[-1] if fresh else table


def core_sum_kernel(y_ref, got_y_ref, y_out, sum_ref):
    sum_ref[...] = y_ref[...] + got_y_ref[...]
    encode_rows(sum_ref, y_out)


def finish_q_kernel(own_ref, got_own_ref, got_ref, gq_out):
    rows = own_ref.shape[0]
    tail = got_ref[rows : rows + TAIL, :].astype(jnp.int32).astype(F32)
    own_tail = got_own_ref[rows:, :].astype(jnp.int32).astype(F32)
    for b in range(rows // BLK):
        at = slice(b * BLK, (b + 1) * BLK)
        own = own_ref[at, :] + decode(got_own_ref[at, :], own_tail[b : b + 1, :])
        gq_out[at, :] = own + decode(got_ref[at, :], tail[b : b + 1, :])


def finish_v_kernel(term_ref, *refs):
    got_terms, (gv_out, gd_out) = refs[:-2], refs[-2:]
    total = term_ref[...]
    dim = total.shape[0]
    for got in got_terms:
        tail = got[dim:, :].astype(jnp.int32).astype(F32)
        total = total + decode(got[0:dim, :], tail[0:1, :])
    local_v = gv_out.shape[0]
    gv_out[...] = total[:, :local_v].T
    gd_out[...] = total[:, local_v:].T


def body(queries, vectors, decoded, mask):
    rows, dim = queries.shape
    local_v = vectors.shape[0]
    blocks = mask.shape[0]
    n = lax.axis_size("qry")
    chunks = n // 4
    wide = 2 * local_v
    scale = 1.0 / math.sqrt(local_v * n)
    pad = -(-blocks // 16) * 16

    def swap(x, bit):
        return lax.ppermute(x, "qry", [(i, i ^ bit) for i in range(n)])

    qm, vd = pl.pallas_call(
        pack_kernel,
        out_shape=(
            jax.ShapeDtypeStruct((rows + pad, dim), BF16),
            jax.ShapeDtypeStruct((wide, dim), BF16),
        ),
        in_specs=[HBM] * 4,
        out_specs=(VMEM, VMEM),
        scratch_shapes=[pltpu.VMEM(mask.shape, mask.dtype), pltpu.SemaphoreType.DMA((4,))],
        compiler_params=params(8),
        name="pack",
    )(*[pltpu.with_memory_space_constraint(x, pltpu.HBM) for x in (queries, vectors, decoded, mask)])
    row_out = jax.ShapeDtypeStruct((rows, dim), F32)
    quarter = chunks // 4
    groups = [tuple(range(g * quarter, (g + 1) * quarter)) for g in range(4)]
    half = 2 * quarter

    def add(sets, which, table, gqs, gvs, send, code_last, name):
        group = sum((groups[g] for g in which), ())
        return grads(
            sets, [vds[s] for s in group], group, chunks, rows, local_v, scale,
            table, gqs, gvs, send, code_last, name,
        )

    qm_y = swap(qm, 2)
    qm_c = swap(qm, 1)
    vds = [vd] + [swap(vd, 4 * s) for s in range(1, chunks)]
    own = [qm, qm_c]
    gq_o, gv0, table = add(own, [0], None, None, None, (), False, "own_0")
    gq_o, gv1, _ = add(own, [1], table, gq_o, None, (), False, "own_1")
    gq_y, gv01, table_y = add([qm_y], [0, 1], None, None, gv0 + gv1, (), False, "y_01")
    qm_y, gq_y, gv01, vds[half:] = lax.optimization_barrier((qm_y, gq_y, gv01, vds[half:]))
    qm_yc = swap(qm_y, 1)
    gq_o, gv23, _ = add(own, [2, 3], table, gq_o, None, (), True, "own_23")
    near, far = tuple(range(1, half)), tuple(range(half, chunks))
    gq_yc, gvs, _ = add([qm_yc], [0, 1, 2, 3], None, None, gv01 + gv23, near, False, "yc")
    got_y = swap(gq_yc[0], 1)
    gq_y, gv23, _ = add([qm_y], [2, 3], table_y, gq_y, gvs[half:], far, False, "y_23")
    got_y, gv01, gv23 = lax.optimization_barrier((got_y, gvs[:half], gv23))
    gq_message = pl.pallas_call(
        core_sum_kernel,
        out_shape=jax.ShapeDtypeStruct((rows + 2 * TAIL, dim), I16),
        in_specs=[VMEM] * 2,
        out_specs=VMEM,
        scratch_shapes=[pltpu.VMEM((rows, dim), F32)],
        compiler_params=params(16),
        name="core_sum",
    )(gq_y[0], got_y)
    gq_own, gq_c = gq_o
    got_own = swap(gq_c, 1)
    term, *messages = gv01 + gv23
    got_message = swap(gq_message, 2)
    got_terms = [swap(x, 4 * s) for s, x in reversed(list(enumerate(messages, 1)))]
    grad_q = pl.pallas_call(
        finish_q_kernel,
        out_shape=row_out,
        in_specs=[VMEM] * 3,
        out_specs=VMEM,
        compiler_params=params(16),
        name="finish_q",
    )(gq_own, got_own, got_message)
    grad_q, term = lax.optimization_barrier((grad_q, term))
    vec_out = jax.ShapeDtypeStruct((local_v, dim), F32)
    grad_v, grad_d = pl.pallas_call(
        finish_v_kernel,
        out_shape=(vec_out, vec_out),
        in_specs=[VMEM] * chunks,
        out_specs=(VMEM,) * 2,
        compiler_params=params(16),
        name="finish_v",
    )(term, *got_terms)
    return grad_q, grad_v, grad_d


def solution(mesh):
    placed = P(("groups", "qry"), None)
    return jax.shard_map(
        body,
        mesh=mesh,
        in_specs=(placed,) * 4,
        out_specs=(placed,) * 3,
        check_vma=False,
    )
```

```python
import math

import jax
import jax.numpy as jnp
from jax import lax
from jax.experimental import pallas as pl
from jax.experimental.pallas import tpu as pltpu
from jax.sharding import PartitionSpec as P

BLK = 256
LOG2E = 1.4426950408889634
LEVELS = 32000.0
TAIL = 16
HEAVY_Y = 1 << 14
HEAVY_TERMS = 9000
VMEM = pl.BlockSpec(memory_space=pltpu.VMEM)
HBM = pl.BlockSpec(memory_space=pltpu.HBM)
F32 = jnp.float32
BF16 = jnp.bfloat16
I16 = jnp.int16


def params(mib):
    return pltpu.CompilerParams(vmem_limit_bytes=mib << 20)


def cost(flops, nbytes):
    return pl.CostEstimate(flops=flops, bytes_accessed=nbytes, transcendentals=0)


def encode(x):
    top = jnp.max(jnp.abs(x), axis=0, keepdims=True)
    exponent = jnp.ceil(jnp.log2(jnp.maximum(top, 1e-30)))
    scaled = jnp.round(x * (jnp.exp2(-exponent) * LEVELS))
    return scaled.astype(jnp.int32).astype(I16), exponent


def decode(x, exponent):
    return x.astype(jnp.int32).astype(F32) * (jnp.exp2(exponent) * (1.0 / LEVELS))


def tail_of(exponents):
    rows = jnp.concatenate(exponents, axis=0)
    rest = jnp.zeros((TAIL - rows.shape[0], rows.shape[1]), F32)
    return jnp.concatenate([rows, rest], axis=0).astype(jnp.int32).astype(I16)


def encode_rows(x_ref, out_ref):
    rows = x_ref.shape[0]
    exponents = []
    for r in range(0, rows, BLK):
        code, exponent = encode(x_ref[r : r + BLK, :])
        out_ref[r : r + BLK, :] = code
        exponents.append(exponent)
    out_ref[rows : rows + TAIL, :] = tail_of(exponents)
    if out_ref.shape[0] > rows + TAIL:
        rest = (out_ref.shape[0] - rows - TAIL, out_ref.shape[1])
        out_ref[rows + TAIL :, :] = jnp.zeros(rest, I16)


def pack_kernel(q_hbm, v_hbm, d_hbm, m_hbm, qm_ref, vd_ref, m_ref, sems):
    rows = q_hbm.shape[0]
    local_v = v_hbm.shape[0]
    copies = [
        pltpu.make_async_copy(m_hbm, m_ref, sems.at[0]),
        pltpu.make_async_copy(v_hbm, vd_ref.at[pl.ds(0, local_v)], sems.at[1]),
        pltpu.make_async_copy(d_hbm, vd_ref.at[pl.ds(local_v, local_v)], sems.at[2]),
        pltpu.make_async_copy(q_hbm, qm_ref.at[pl.ds(0, rows)], sems.at[3]),
    ]
    for copy in copies:
        copy.start()
    copies[0].wait()
    blocks, cols = m_ref.shape
    pad, lanes = qm_ref.shape[0] - rows, qm_ref.shape[1]
    flags = jnp.concatenate([m_ref[...].astype(F32), jnp.zeros((blocks, lanes - cols), F32)], axis=1)
    flags = jnp.concatenate([flags, jnp.zeros((pad - blocks, lanes), F32)], axis=0)
    qm_ref[rows:, :] = flags.astype(BF16)
    for copy in copies[1:]:
        copy.wait()


def live_table(flags, chunks, local_v, scale):
    me = lax.axis_index("qry")
    lanes = flags.shape[1]
    rows = lax.broadcasted_iota(jnp.int32, (lanes, 128), 0)
    cols = [(jnp.bitwise_xor(me, 4 * s) * local_v) // BLK for s in range(chunks)]
    onehot = jnp.concatenate([(rows == col).astype(F32) for col in cols], axis=1)
    return jnp.dot(flags, onehot.astype(BF16), preferred_element_type=F32) * (-2.0 * scale)


def tile_weights(q, w, live, chunks, local_v):
    wide = 2 * local_v
    both = lax.dot_general(q, w, (((1,), (1,)), ((), ())), preferred_element_type=F32)
    row_blocks = []
    for b in range(q.shape[0] // BLK):
        weights = []
        for c in range(chunks):
            score = both[b * BLK : (b + 1) * BLK, c * wide : c * wide + local_v]
            error = score - both[b * BLK : (b + 1) * BLK, c * wide + local_v : (c + 1) * wide]
            sig = 1.0 / (1.0 + jnp.exp2(score * (-LOG2E)))
            neg = (error * live(b, c)) * sig
            pos = neg * (error * (0.5 * sig - 0.5) - 1.0)
            weights += [pos.astype(BF16), neg.astype(BF16)]
        row_blocks.append(jnp.concatenate(weights, axis=1))
    return jnp.concatenate(row_blocks, axis=0)


def grads(sets, vds, group, chunks, rows, local_v, scale, table, gqs, gvs, send, code_last, name, weight):
    k, m = len(sets), len(vds)
    dim = sets[0].shape[1]
    pad = sets[0].shape[0] - rows
    wide = 2 * local_v
    part = min(m, 4)
    height = 2 * BLK if rows % (2 * BLK) == 0 else BLK
    fresh = table is None

    def kernel(*refs):
        qm_refs, refs = refs[:k], refs[k:]
        vd_refs, refs = refs[:m], refs[m:]
        gq_ins, gv_ins = None, None
        if not fresh:
            table_ref, refs = refs[0], refs[1:]
        if gqs is not None:
            gq_ins, refs = refs[:k], refs[k:]
        if gvs is not None:
            gv_ins, refs = refs[:m], refs[m:]
        gq_refs, refs = refs[:k], refs[k:]
        gv_outs, refs = refs[:m], refs[m:]
        if fresh:
            table_ref, refs = refs[0], refs[1:]
            for t in range(k):
                table = live_table(qm_refs[t][rows:, :], chunks, local_v, scale)
                for s in range(chunks):
                    table_ref[s, t * pad : (t + 1) * pad, :] = table[:, s * 128 : (s + 1) * 128]
        gv_ref, w_ref, last_ref = refs
        for s in range(m):
            w_ref[s * wide : (s + 1) * wide, :] = vd_refs[s][...]
            gv_ref[:, s * wide : (s + 1) * wide] = (
                jnp.zeros((dim, wide), F32) if gv_ins is None else gv_ins[s][...]
            )
        outs = [*gq_refs[: k - 1], last_ref if code_last else gq_refs[k - 1]]

        def tile(t, r0, first):
            def live(b, c):
                s = group[first + c]
                return table_ref[s, pl.ds(t * pad + r0 // BLK + b, 1), :]

            w = w_ref[first * wide : (first + part) * wide, :]
            weights = tile_weights(qm_refs[t][pl.ds(r0, height), :], w, live, part, local_v)
            gq = jnp.dot(weights, w, preferred_element_type=F32)
            if first > 0:
                gq = gq + outs[t][pl.ds(r0, height), :]
            elif gq_ins is not None:
                gq = gq + gq_ins[t][pl.ds(r0, height), :]
            outs[t][pl.ds(r0, height), :] = gq
            return weights

        if m <= 4:
            weights = [tile(t, r0, 0) for t in range(k) for r0 in range(0, rows, height)]
            q = jnp.concatenate([ref[0:rows, :] for ref in qm_refs], axis=0)
            gv_ref[...] += jnp.dot(
                q.T, jnp.concatenate(weights, axis=0), preferred_element_type=F32
            )
        else:
            for t in range(k):
                for first in range(0, m, part):

                    def step(i, carry, t=t, first=first):
                        r0 = pl.multiple_of(i * height, height)
                        weights = tile(t, r0, first)
                        q = qm_refs[t][pl.ds(r0, height), :]
                        gv_ref[:, first * wide : (first + part) * wide] += jnp.dot(
                            q.T, weights, preferred_element_type=F32
                        )
                        return carry

                    lax.fori_loop(0, rows // height, step, 0)
        if code_last:
            encode_rows(last_ref, gq_refs[k - 1])
        for s in range(m):
            term = gv_ref[:, s * wide : (s + 1) * wide]
            if group[s] in send:
                code, exponent = encode(term)
                gv_outs[s][0:dim, :] = code
                gv_outs[s][dim:, :] = tail_of([exponent])
            else:
                gv_outs[s][...] = term

    operands = [*sets, *vds, *([] if fresh else [table]), *(gqs or []), *(gvs or [])]
    outs = [jax.ShapeDtypeStruct((rows, dim), F32)] * k + [
        jax.ShapeDtypeStruct((dim + TAIL, wide), I16)
        if s in send
        else jax.ShapeDtypeStruct((dim, wide), F32)
        for s in group
    ]
    if code_last:
        outs[k - 1] = jax.ShapeDtypeStruct((rows + TAIL, dim), I16)
    if fresh:
        outs.append(jax.ShapeDtypeStruct((chunks, k * pad, 128), F32))
    res = pl.pallas_call(
        kernel,
        out_shape=tuple(outs),
        in_specs=[VMEM] * len(operands),
        out_specs=(VMEM,) * len(outs),
        scratch_shapes=[
            pltpu.VMEM((dim, m * wide), F32),
            pltpu.VMEM((m * wide, dim), BF16),
            pltpu.VMEM((rows if code_last else 8, dim), F32),
        ],
        compiler_params=params(32),
        cost_estimate=cost(weight * k * rows * m * wide, 1 << 10),
        name=name,
    )(*operands)
    return list(res[:k]), list(res[k : k + m]), res[-1] if fresh else table


def core_sum_kernel(y_ref, got_y_ref, y_out, sum_ref):
    sum_ref[...] = y_ref[...] + got_y_ref[...]
    encode_rows(sum_ref, y_out)


def finish_q_kernel(own_ref, got_own_ref, got_ref, gq_out):
    rows = own_ref.shape[0]
    tail = got_ref[rows : rows + TAIL, :].astype(jnp.int32).astype(F32)
    own_tail = got_own_ref[rows:, :].astype(jnp.int32).astype(F32)
    for b in range(rows // BLK):
        at = slice(b * BLK, (b + 1) * BLK)
        own = own_ref[at, :] + decode(got_own_ref[at, :], own_tail[b : b + 1, :])
        gq_out[at, :] = own + decode(got_ref[at, :], tail[b : b + 1, :])


def sum_terms(term_ref, got_terms):
    total = term_ref[...]
    dim = total.shape[0]
    for got in got_terms:
        tail = got[dim:, :].astype(jnp.int32).astype(F32)
        total = total + decode(got[0:dim, :], tail[0:1, :])
    return total


def add_terms_kernel(term_ref, *refs):
    refs[-1][...] = sum_terms(term_ref, refs[:-1])


def finish_v_kernel(term_ref, *refs):
    gv_out, gd_out = refs[-2:]
    total = sum_terms(term_ref, refs[:-2])
    local_v = gv_out.shape[0]
    gv_out[...] = total[:, :local_v].T
    gd_out[...] = total[:, local_v:].T


def body(queries, vectors, decoded, mask):
    rows, dim = queries.shape
    local_v = vectors.shape[0]
    blocks = mask.shape[0]
    n = lax.axis_size("qry")
    chunks = n // 4
    wide = 2 * local_v
    scale = 1.0 / math.sqrt(local_v * n)
    pad = -(-blocks // 16) * 16

    def swap(x, bit):
        return lax.ppermute(x, "qry", [(i, i ^ bit) for i in range(n)])

    qm, vd = pl.pallas_call(
        pack_kernel,
        out_shape=(
            jax.ShapeDtypeStruct((rows + pad, dim), BF16),
            jax.ShapeDtypeStruct((wide, dim), BF16),
        ),
        in_specs=[HBM] * 4,
        out_specs=(VMEM, VMEM),
        scratch_shapes=[pltpu.VMEM(mask.shape, mask.dtype), pltpu.SemaphoreType.DMA((4,))],
        compiler_params=params(8),
        name="pack",
    )(*[pltpu.with_memory_space_constraint(x, pltpu.HBM) for x in (queries, vectors, decoded, mask)])
    row_out = jax.ShapeDtypeStruct((rows, dim), F32)
    quarter = chunks // 4
    groups = [tuple(range(g * quarter, (g + 1) * quarter)) for g in range(4)]
    half = 2 * quarter

    def add(sets, which, table, gqs, gvs, send, name, code_last=False, weight=1):
        group = sum((groups[g] for g in which), ())
        return grads(
            sets, [vds[s] for s in group], group, chunks, rows, local_v, scale,
            table, gqs, gvs, send, code_last, name, weight,
        )

    qm_y = swap(qm, 2)
    qm_c = swap(qm, 1)
    vds = [vd] + [swap(vd, 4 * s) for s in range(1, chunks)]
    own = [qm, qm_c]
    near, far = tuple(range(1, half)), tuple(range(half, chunks))
    gq_o, gv0, table = add(own, [0], None, None, None, (), "own_0")
    gq_o, gv1, _ = add(own, [1], table, gq_o, None, (), "own_1")
    qm_y, gv1 = lax.optimization_barrier((qm_y, gv1))
    qm_yc = swap(qm_y, 1)
    gq_y, gv01, table_y = add([qm_y], [0, 1], None, None, gv0 + gv1, (), "y_01", weight=HEAVY_Y)
    gq_yc, gv01, table_yc = add([qm_yc], [0, 1], None, None, gv01, near, "yc_01")
    gq_yc, gv01, vds[half:] = lax.optimization_barrier((gq_yc, gv01, vds[half:]))
    gq_yc, gv23, _ = add([qm_yc], [2, 3], table_yc, gq_yc, None, (), "yc_23")
    got_y = swap(gq_yc[0], 1)
    gq_y, gv23, _ = add([qm_y], [2, 3], table_y, gq_y, gv23, (), "y_23")
    gq_o, gv23, _ = add(own, [2, 3], table, gq_o, gv23, far, "own_23", code_last=True)
    got_y, gv01, gv23 = lax.optimization_barrier((got_y, gv01, gv23))
    gq_message = pl.pallas_call(
        core_sum_kernel,
        out_shape=jax.ShapeDtypeStruct((rows + 2 * TAIL, dim), I16),
        in_specs=[VMEM] * 2,
        out_specs=VMEM,
        scratch_shapes=[pltpu.VMEM((rows, dim), F32)],
        compiler_params=params(16),
        name="core_sum",
    )(gq_y[0], got_y)
    gq_own, gq_c = gq_o
    got_own = swap(gq_c, 1)
    term, *messages = gv01 + gv23
    got_message = swap(gq_message, 2)
    got_terms = [swap(x, 4 * s) for s, x in reversed(list(enumerate(messages, 1)))]
    first, rest = got_terms[:quarter], got_terms[quarter:]
    term = pl.pallas_call(
        add_terms_kernel,
        out_shape=jax.ShapeDtypeStruct((dim, wide), F32),
        in_specs=[VMEM] * (1 + len(first)),
        out_specs=VMEM,
        compiler_params=params(16),
        cost_estimate=cost(HEAVY_TERMS * rows * wide, 1 << 10),
        name="add_terms",
    )(term, *first)
    gq_own, term = lax.optimization_barrier((gq_own, term))
    grad_q = pl.pallas_call(
        finish_q_kernel,
        out_shape=row_out,
        in_specs=[VMEM] * 3,
        out_specs=VMEM,
        compiler_params=params(16),
        name="finish_q",
    )(gq_own, got_own, got_message)
    grad_q, term = lax.optimization_barrier((grad_q, term))
    vec_out = jax.ShapeDtypeStruct((local_v, dim), F32)
    grad_v, grad_d = pl.pallas_call(
        finish_v_kernel,
        out_shape=(vec_out, vec_out),
        in_specs=[VMEM] * (1 + len(rest)),
        out_specs=(VMEM,) * 2,
        compiler_params=params(16),
        name="finish_v",
    )(term, *rest)
    return grad_q, grad_v, grad_d


def solution(mesh):
    placed = P(("groups", "qry"), None)
    return jax.shard_map(
        body,
        mesh=mesh,
        in_specs=(placed,) * 4,
        out_specs=(placed,) * 3,
        check_vma=False,
    )
```

```python
import math

import jax
import jax.numpy as jnp
from jax import lax
from jax.experimental import pallas as pl
from jax.experimental.pallas import tpu as pltpu
from jax.sharding import PartitionSpec as P

BLK = 256
LOG2E = 1.4426950408889634
LEVELS = 32000.0
TAIL = 16
HEAVY = 1 << 14
VMEM = pl.BlockSpec(memory_space=pltpu.VMEM)
HBM = pl.BlockSpec(memory_space=pltpu.HBM)
F32 = jnp.float32
BF16 = jnp.bfloat16
I16 = jnp.int16


def params(mib):
    return pltpu.CompilerParams(vmem_limit_bytes=mib << 20)


def cost(flops, nbytes):
    return pl.CostEstimate(flops=flops, bytes_accessed=nbytes, transcendentals=0)


def encode(x):
    top = jnp.max(jnp.abs(x), axis=0, keepdims=True)
    exponent = jnp.ceil(jnp.log2(jnp.maximum(top, 1e-30)))
    scaled = jnp.round(x * (jnp.exp2(-exponent) * LEVELS))
    return scaled.astype(jnp.int32).astype(I16), exponent


def decode(x, exponent):
    return x.astype(jnp.int32).astype(F32) * (jnp.exp2(exponent) * (1.0 / LEVELS))


def tail_of(exponents):
    rows = jnp.concatenate(exponents, axis=0)
    rest = jnp.zeros((TAIL - rows.shape[0], rows.shape[1]), F32)
    return jnp.concatenate([rows, rest], axis=0).astype(jnp.int32).astype(I16)


def encode_rows(x_ref, out_ref):
    rows = x_ref.shape[0]
    exponents = []
    for r in range(0, rows, BLK):
        code, exponent = encode(x_ref[r : r + BLK, :])
        out_ref[r : r + BLK, :] = code
        exponents.append(exponent)
    out_ref[rows : rows + TAIL, :] = tail_of(exponents)
    if out_ref.shape[0] > rows + TAIL:
        rest = (out_ref.shape[0] - rows - TAIL, out_ref.shape[1])
        out_ref[rows + TAIL :, :] = jnp.zeros(rest, I16)


def pack_kernel(q_hbm, v_hbm, d_hbm, m_hbm, qm_ref, vd_ref, m_ref, sems):
    rows = q_hbm.shape[0]
    local_v = v_hbm.shape[0]
    copies = [
        pltpu.make_async_copy(m_hbm, m_ref, sems.at[0]),
        pltpu.make_async_copy(v_hbm, vd_ref.at[pl.ds(0, local_v)], sems.at[1]),
        pltpu.make_async_copy(d_hbm, vd_ref.at[pl.ds(local_v, local_v)], sems.at[2]),
        pltpu.make_async_copy(q_hbm, qm_ref.at[pl.ds(0, rows)], sems.at[3]),
    ]
    for copy in copies:
        copy.start()
    copies[0].wait()
    blocks, cols = m_ref.shape
    pad, lanes = qm_ref.shape[0] - rows, qm_ref.shape[1]
    flags = jnp.concatenate([m_ref[...].astype(F32), jnp.zeros((blocks, lanes - cols), F32)], axis=1)
    flags = jnp.concatenate([flags, jnp.zeros((pad - blocks, lanes), F32)], axis=0)
    qm_ref[rows:, :] = flags.astype(BF16)
    for copy in copies[1:]:
        copy.wait()


def live_table(flags, chunks, local_v, scale):
    me = lax.axis_index("qry")
    lanes = flags.shape[1]
    rows = lax.broadcasted_iota(jnp.int32, (lanes, 128), 0)
    cols = [(jnp.bitwise_xor(me, 4 * s) * local_v) // BLK for s in range(chunks)]
    onehot = jnp.concatenate([(rows == col).astype(F32) for col in cols], axis=1)
    return jnp.dot(flags, onehot.astype(BF16), preferred_element_type=F32) * (-2.0 * scale)


def tile_weights(q, w, live, chunks, local_v):
    wide = 2 * local_v
    both = lax.dot_general(q, w, (((1,), (1,)), ((), ())), preferred_element_type=F32)
    row_blocks = []
    for b in range(q.shape[0] // BLK):
        weights = []
        for c in range(chunks):
            score = both[b * BLK : (b + 1) * BLK, c * wide : c * wide + local_v]
            error = score - both[b * BLK : (b + 1) * BLK, c * wide + local_v : (c + 1) * wide]
            sig = 1.0 / (1.0 + jnp.exp2(score * (-LOG2E)))
            neg = (error * live(b, c)) * sig
            pos = neg * (error * (0.5 * sig - 0.5) - 1.0)
            weights += [pos.astype(BF16), neg.astype(BF16)]
        row_blocks.append(jnp.concatenate(weights, axis=1))
    return jnp.concatenate(row_blocks, axis=0)


def grads(sets, vds, group, chunks, rows, local_v, scale, table, gqs, gvs, send, code_last, name, weight):
    k, m = len(sets), len(vds)
    dim = sets[0].shape[1]
    pad = sets[0].shape[0] - rows
    wide = 2 * local_v
    part = min(m, 4)
    height = 2 * BLK if rows % (2 * BLK) == 0 else BLK
    fresh = table is None

    def kernel(*refs):
        qm_refs, refs = refs[:k], refs[k:]
        vd_refs, refs = refs[:m], refs[m:]
        gq_ins, gv_ins = None, None
        if not fresh:
            table_ref, refs = refs[0], refs[1:]
        if gqs is not None:
            gq_ins, refs = refs[:k], refs[k:]
        if gvs is not None:
            gv_ins, refs = refs[:m], refs[m:]
        gq_refs, refs = refs[:k], refs[k:]
        gv_outs, refs = refs[:m], refs[m:]
        if fresh:
            table_ref, refs = refs[0], refs[1:]
            for t in range(k):
                table = live_table(qm_refs[t][rows:, :], chunks, local_v, scale)
                for s in range(chunks):
                    table_ref[s, t * pad : (t + 1) * pad, :] = table[:, s * 128 : (s + 1) * 128]
        gv_ref, w_ref, last_ref = refs
        for s in range(m):
            w_ref[s * wide : (s + 1) * wide, :] = vd_refs[s][...]
            gv_ref[:, s * wide : (s + 1) * wide] = (
                jnp.zeros((dim, wide), F32) if gv_ins is None else gv_ins[s][...]
            )
        outs = [*gq_refs[: k - 1], last_ref if code_last else gq_refs[k - 1]]

        def tile(t, r0, first):
            def live(b, c):
                s = group[first + c]
                return table_ref[s, pl.ds(t * pad + r0 // BLK + b, 1), :]

            w = w_ref[first * wide : (first + part) * wide, :]
            weights = tile_weights(qm_refs[t][pl.ds(r0, height), :], w, live, part, local_v)
            gq = jnp.dot(weights, w, preferred_element_type=F32)
            if first > 0:
                gq = gq + outs[t][pl.ds(r0, height), :]
            elif gq_ins is not None:
                gq = gq + gq_ins[t][pl.ds(r0, height), :]
            outs[t][pl.ds(r0, height), :] = gq
            return weights

        if m <= 4:
            weights = [tile(t, r0, 0) for t in range(k) for r0 in range(0, rows, height)]
            q = jnp.concatenate([ref[0:rows, :] for ref in qm_refs], axis=0)
            gv_ref[...] += jnp.dot(
                q.T, jnp.concatenate(weights, axis=0), preferred_element_type=F32
            )
        else:
            for t in range(k):
                for first in range(0, m, part):

                    def step(i, carry, t=t, first=first):
                        r0 = pl.multiple_of(i * height, height)
                        weights = tile(t, r0, first)
                        q = qm_refs[t][pl.ds(r0, height), :]
                        gv_ref[:, first * wide : (first + part) * wide] += jnp.dot(
                            q.T, weights, preferred_element_type=F32
                        )
                        return carry

                    lax.fori_loop(0, rows // height, step, 0)
        if code_last:
            encode_rows(last_ref, gq_refs[k - 1])
        for s in range(m):
            term = gv_ref[:, s * wide : (s + 1) * wide]
            if group[s] in send:
                code, exponent = encode(term)
                gv_outs[s][0:dim, :] = code
                gv_outs[s][dim:, :] = tail_of([exponent])
            else:
                gv_outs[s][...] = term

    operands = [*sets, *vds, *([] if fresh else [table]), *(gqs or []), *(gvs or [])]
    outs = [jax.ShapeDtypeStruct((rows, dim), F32)] * k + [
        jax.ShapeDtypeStruct((dim + TAIL, wide), I16)
        if s in send
        else jax.ShapeDtypeStruct((dim, wide), F32)
        for s in group
    ]
    if code_last:
        outs[k - 1] = jax.ShapeDtypeStruct((rows + TAIL, dim), I16)
    if fresh:
        outs.append(jax.ShapeDtypeStruct((chunks, k * pad, 128), F32))
    res = pl.pallas_call(
        kernel,
        out_shape=tuple(outs),
        in_specs=[VMEM] * len(operands),
        out_specs=(VMEM,) * len(outs),
        scratch_shapes=[
            pltpu.VMEM((dim, m * wide), F32),
            pltpu.VMEM((m * wide, dim), BF16),
            pltpu.VMEM((rows if code_last else 8, dim), F32),
        ],
        compiler_params=params(32),
        cost_estimate=cost(weight * k * rows * m * wide, 1 << 10),
        name=name,
    )(*operands)
    return list(res[:k]), list(res[k : k + m]), res[-1] if fresh else table


def core_sum_kernel(y_ref, got_y_ref, y_out, sum_ref):
    sum_ref[...] = y_ref[...] + got_y_ref[...]
    encode_rows(sum_ref, y_out)


def finish_q_kernel(own_ref, got_own_ref, got_ref, gq_out):
    rows = own_ref.shape[0]
    tail = got_ref[rows : rows + TAIL, :].astype(jnp.int32).astype(F32)
    own_tail = got_own_ref[rows:, :].astype(jnp.int32).astype(F32)
    for b in range(rows // BLK):
        at = slice(b * BLK, (b + 1) * BLK)
        own = own_ref[at, :] + decode(got_own_ref[at, :], own_tail[b : b + 1, :])
        gq_out[at, :] = own + decode(got_ref[at, :], tail[b : b + 1, :])


def finish_v_kernel(term_ref, *refs):
    got_terms, (gv_out, gd_out) = refs[:-2], refs[-2:]
    total = term_ref[...]
    dim = total.shape[0]
    for got in got_terms:
        tail = got[dim:, :].astype(jnp.int32).astype(F32)
        total = total + decode(got[0:dim, :], tail[0:1, :])
    local_v = gv_out.shape[0]
    gv_out[...] = total[:, :local_v].T
    gd_out[...] = total[:, local_v:].T


def body(queries, vectors, decoded, mask):
    rows, dim = queries.shape
    local_v = vectors.shape[0]
    blocks = mask.shape[0]
    n = lax.axis_size("qry")
    chunks = n // 4
    wide = 2 * local_v
    scale = 1.0 / math.sqrt(local_v * n)
    pad = -(-blocks // 16) * 16

    def swap(x, bit):
        return lax.ppermute(x, "qry", [(i, i ^ bit) for i in range(n)])

    qm, vd = pl.pallas_call(
        pack_kernel,
        out_shape=(
            jax.ShapeDtypeStruct((rows + pad, dim), BF16),
            jax.ShapeDtypeStruct((wide, dim), BF16),
        ),
        in_specs=[HBM] * 4,
        out_specs=(VMEM, VMEM),
        scratch_shapes=[pltpu.VMEM(mask.shape, mask.dtype), pltpu.SemaphoreType.DMA((4,))],
        compiler_params=params(8),
        name="pack",
    )(*[pltpu.with_memory_space_constraint(x, pltpu.HBM) for x in (queries, vectors, decoded, mask)])
    row_out = jax.ShapeDtypeStruct((rows, dim), F32)
    quarter = chunks // 4
    groups = [tuple(range(g * quarter, (g + 1) * quarter)) for g in range(4)]
    half = 2 * quarter

    def add(sets, which, table, gqs, gvs, send, name, code_last=False, weight=1):
        group = sum((groups[g] for g in which), ())
        return grads(
            sets, [vds[s] for s in group], group, chunks, rows, local_v, scale,
            table, gqs, gvs, send, code_last, name, weight,
        )

    qm_y = swap(qm, 2)
    qm_c = swap(qm, 1)
    vds = [vd] + [swap(vd, 4 * s) for s in range(1, chunks)]
    own = [qm, qm_c]
    near, far = tuple(range(1, half)), tuple(range(half, chunks))
    gq_o, gv0, table = add(own, [0], None, None, None, (), "own_0")
    gq_o, gv1, _ = add(own, [1], table, gq_o, None, (), "own_1")
    qm_y, gv1 = lax.optimization_barrier((qm_y, gv1))
    qm_yc = swap(qm_y, 1)
    gq_y, gv01, table_y = add([qm_y], [0, 1], None, None, gv0 + gv1, (), "y_01", weight=HEAVY)
    gq_yc, gv01, table_yc = add([qm_yc], [0, 1], None, None, gv01, near, "yc_01")
    gq_yc, gv01, late = lax.optimization_barrier((gq_yc, gv01, vds[half:][::-1]))
    vds[half:] = late[::-1]
    gq_yc, gv23, _ = add([qm_yc], [2, 3], table_yc, gq_yc, None, (), "yc_23")
    got_y = swap(gq_yc[0], 1)
    gq_y, gv23, _ = add([qm_y], [2, 3], table_y, gq_y, gv23, (), "y_23")
    gq_o, gv23, _ = add(own, [2, 3], table, gq_o, gv23, far, "own_23", code_last=True)
    got_y, gv01, gv23 = lax.optimization_barrier((got_y, gv01, gv23))
    gq_message = pl.pallas_call(
        core_sum_kernel,
        out_shape=jax.ShapeDtypeStruct((rows + 2 * TAIL, dim), I16),
        in_specs=[VMEM] * 2,
        out_specs=VMEM,
        scratch_shapes=[pltpu.VMEM((rows, dim), F32)],
        compiler_params=params(16),
        name="core_sum",
    )(gq_y[0], got_y)
    gq_own, gq_c = gq_o
    got_own = swap(gq_c, 1)
    term, *messages = gv01 + gv23
    got_message = swap(gq_message, 2)
    order = sorted(range(1, chunks), key=lambda s: (s < half, s))
    got_terms = [swap(messages[s - 1], 4 * s) for s in order]
    grad_q = pl.pallas_call(
        finish_q_kernel,
        out_shape=row_out,
        in_specs=[VMEM] * 3,
        out_specs=VMEM,
        compiler_params=params(16),
        name="finish_q",
    )(gq_own, got_own, got_message)
    grad_q, term = lax.optimization_barrier((grad_q, term))
    vec_out = jax.ShapeDtypeStruct((local_v, dim), F32)
    grad_v, grad_d = pl.pallas_call(
        finish_v_kernel,
        out_shape=(vec_out, vec_out),
        in_specs=[VMEM] * chunks,
        out_specs=(VMEM,) * 2,
        compiler_params=params(16),
        name="finish_v",
    )(term, *got_terms)
    return grad_q, grad_v, grad_d


def solution(mesh):
    placed = P(("groups", "qry"), None)
    return jax.shard_map(
        body,
        mesh=mesh,
        in_specs=(placed,) * 4,
        out_specs=(placed,) * 3,
        check_vma=False,
    )
```

```python
import math

import jax
import jax.numpy as jnp
from jax import lax
from jax.experimental import pallas as pl
from jax.experimental.pallas import tpu as pltpu
from jax.sharding import PartitionSpec as P

BLK = 256
LOG2E = 1.4426950408889634
LEVELS = 32000.0
TAIL = 16
HEAVY = 1 << 14
MEDIUM = 1500
VMEM = pl.BlockSpec(memory_space=pltpu.VMEM)
HBM = pl.BlockSpec(memory_space=pltpu.HBM)
F32 = jnp.float32
BF16 = jnp.bfloat16
I16 = jnp.int16


def params(mib):
    return pltpu.CompilerParams(vmem_limit_bytes=mib << 20)


def cost(flops, nbytes):
    return pl.CostEstimate(flops=flops, bytes_accessed=nbytes, transcendentals=0)


def encode(x):
    top = jnp.max(jnp.abs(x), axis=0, keepdims=True)
    exponent = jnp.ceil(jnp.log2(jnp.maximum(top, 1e-30)))
    scaled = jnp.round(x * (jnp.exp2(-exponent) * LEVELS))
    return scaled.astype(jnp.int32).astype(I16), exponent


def decode(x, exponent):
    return x.astype(jnp.int32).astype(F32) * (jnp.exp2(exponent) * (1.0 / LEVELS))


def tail_of(exponents):
    rows = jnp.concatenate(exponents, axis=0)
    rest = jnp.zeros((TAIL - rows.shape[0], rows.shape[1]), F32)
    return jnp.concatenate([rows, rest], axis=0).astype(jnp.int32).astype(I16)


def encode_rows(x_ref, out_ref):
    rows = x_ref.shape[0]
    exponents = []
    for r in range(0, rows, BLK):
        code, exponent = encode(x_ref[r : r + BLK, :])
        out_ref[r : r + BLK, :] = code
        exponents.append(exponent)
    out_ref[rows : rows + TAIL, :] = tail_of(exponents)
    if out_ref.shape[0] > rows + TAIL:
        rest = (out_ref.shape[0] - rows - TAIL, out_ref.shape[1])
        out_ref[rows + TAIL :, :] = jnp.zeros(rest, I16)


def pack_kernel(q_hbm, v_hbm, d_hbm, m_hbm, q_ref, vd_ref, flags_ref, m_ref, sems):
    local_v = v_hbm.shape[0]
    copies = [
        pltpu.make_async_copy(m_hbm, m_ref, sems.at[0]),
        pltpu.make_async_copy(v_hbm, vd_ref.at[pl.ds(0, local_v)], sems.at[1]),
        pltpu.make_async_copy(d_hbm, vd_ref.at[pl.ds(local_v, local_v)], sems.at[2]),
        pltpu.make_async_copy(q_hbm, q_ref, sems.at[3]),
    ]
    for copy in copies:
        copy.start()
    copies[0].wait()
    blocks, cols = m_ref.shape
    pad, lanes = flags_ref.shape
    flags = jnp.concatenate([m_ref[...].astype(F32), jnp.zeros((blocks, lanes - cols), F32)], axis=1)
    if pad > blocks:
        flags = jnp.concatenate([flags, jnp.zeros((pad - blocks, lanes), F32)], axis=0)
    flags_ref[...] = flags.astype(BF16)
    for copy in copies[1:]:
        copy.wait()


def live_table(flags, chunks, local_v, scale):
    me = lax.axis_index("qry")
    lanes = flags.shape[1]
    rows = lax.broadcasted_iota(jnp.int32, (lanes, 128), 0)
    cols = [(jnp.bitwise_xor(me, 4 * s) * local_v) // BLK for s in range(chunks)]
    onehot = jnp.concatenate([(rows == col).astype(F32) for col in cols], axis=1)
    return jnp.dot(flags, onehot.astype(BF16), preferred_element_type=F32) * (-2.0 * scale)


def tile_weights(q, w, live, chunks, local_v):
    wide = 2 * local_v
    both = lax.dot_general(q, w, (((1,), (1,)), ((), ())), preferred_element_type=F32)
    row_blocks = []
    for b in range(q.shape[0] // BLK):
        weights = []
        for c in range(chunks):
            score = both[b * BLK : (b + 1) * BLK, c * wide : c * wide + local_v]
            error = score - both[b * BLK : (b + 1) * BLK, c * wide + local_v : (c + 1) * wide]
            sig = 1.0 / (1.0 + jnp.exp2(score * (-LOG2E)))
            neg = (error * live(b, c)) * sig
            pos = neg * (error * (0.5 * sig - 0.5) - 1.0)
            weights += [pos.astype(BF16), neg.astype(BF16)]
        row_blocks.append(jnp.concatenate(weights, axis=1))
    return jnp.concatenate(row_blocks, axis=0)


def grads(sets, vds, group, chunks, rows, local_v, scale, table, row0, flags, gqs, gvs, send, code_last, name, weight):
    k, m = len(sets), len(vds)
    dim = sets[0].shape[1]
    fresh = table is None
    pad = (sum(x.shape[0] for x in flags) if fresh else table.shape[1]) // 2
    wide = 2 * local_v
    part = min(m, 4)
    height = 2 * BLK if rows % (2 * BLK) == 0 else BLK

    def kernel(*refs):
        qm_refs, refs = refs[:k], refs[k:]
        vd_refs, refs = refs[:m], refs[m:]
        gq_ins, gv_ins = None, None
        if not fresh:
            table_ref, refs = refs[0], refs[1:]
        else:
            flags_refs, refs = refs[: len(flags)], refs[len(flags) :]
        if gqs is not None:
            gq_ins, refs = refs[:k], refs[k:]
        if gvs is not None:
            gv_ins, refs = refs[:m], refs[m:]
        gq_refs, refs = refs[:k], refs[k:]
        gv_outs, refs = refs[:m], refs[m:]
        if fresh:
            table_ref, refs = refs[0], refs[1:]
            both = jnp.concatenate([ref[...] for ref in flags_refs], axis=0)
            if len(flags) == 2:
                refs[0][...] = both
                refs = refs[1:]
            lanes = live_table(both, chunks, local_v, scale)
            for s in range(chunks):
                table_ref[s, :, :] = lanes[:, s * 128 : (s + 1) * 128]
        gv_ref, w_ref, last_ref = refs
        for s in range(m):
            w_ref[s * wide : (s + 1) * wide, :] = vd_refs[s][...]
            gv_ref[:, s * wide : (s + 1) * wide] = (
                jnp.zeros((dim, wide), F32) if gv_ins is None else gv_ins[s][...]
            )
        outs = [*gq_refs[: k - 1], last_ref if code_last else gq_refs[k - 1]]

        def tile(t, r0, first):
            def live(b, c):
                s = group[first + c]
                return table_ref[s, pl.ds(row0 + t * pad + r0 // BLK + b, 1), :]

            w = w_ref[first * wide : (first + part) * wide, :]
            weights = tile_weights(qm_refs[t][pl.ds(r0, height), :], w, live, part, local_v)
            gq = jnp.dot(weights, w, preferred_element_type=F32)
            if first > 0:
                gq = gq + outs[t][pl.ds(r0, height), :]
            elif gq_ins is not None:
                gq = gq + gq_ins[t][pl.ds(r0, height), :]
            outs[t][pl.ds(r0, height), :] = gq
            return weights

        if m <= 4:
            weights = [tile(t, r0, 0) for t in range(k) for r0 in range(0, rows, height)]
            q = jnp.concatenate([ref[0:rows, :] for ref in qm_refs], axis=0)
            gv_ref[...] += jnp.dot(
                q.T, jnp.concatenate(weights, axis=0), preferred_element_type=F32
            )
        else:
            for t in range(k):
                for first in range(0, m, part):

                    def step(i, carry, t=t, first=first):
                        r0 = pl.multiple_of(i * height, height)
                        weights = tile(t, r0, first)
                        q = qm_refs[t][pl.ds(r0, height), :]
                        gv_ref[:, first * wide : (first + part) * wide] += jnp.dot(
                            q.T, weights, preferred_element_type=F32
                        )
                        return carry

                    lax.fori_loop(0, rows // height, step, 0)
        if code_last:
            encode_rows(last_ref, gq_refs[k - 1])
        for s in range(m):
            term = gv_ref[:, s * wide : (s + 1) * wide]
            if group[s] in send:
                code, exponent = encode(term)
                gv_outs[s][0:dim, :] = code
                gv_outs[s][dim:, :] = tail_of([exponent])
            else:
                gv_outs[s][...] = term

    given = flags if fresh else [table]
    operands = [*sets, *vds, *given, *(gqs or []), *(gvs or [])]
    outs = [jax.ShapeDtypeStruct((rows, dim), F32)] * k + [
        jax.ShapeDtypeStruct((dim + TAIL, wide), I16)
        if s in send
        else jax.ShapeDtypeStruct((dim, wide), F32)
        for s in group
    ]
    if code_last:
        outs[k - 1] = jax.ShapeDtypeStruct((rows + TAIL, dim), I16)
    if fresh:
        outs.append(jax.ShapeDtypeStruct((chunks, 2 * pad, 128), F32))
        if len(flags) == 2:
            outs.append(jax.ShapeDtypeStruct((2 * pad, dim), BF16))
    res = pl.pallas_call(
        kernel,
        out_shape=tuple(outs),
        in_specs=[VMEM] * len(operands),
        out_specs=(VMEM,) * len(outs),
        scratch_shapes=[
            pltpu.VMEM((dim, m * wide), F32),
            pltpu.VMEM((m * wide, dim), BF16),
            pltpu.VMEM((rows if code_last else 8, dim), F32),
        ],
        compiler_params=params(32),
        cost_estimate=cost(weight * k * rows * m * wide, 1 << 10),
        name=name,
    )(*operands)
    return list(res[:k]), list(res[k : k + m]), res[k + m :]


def core_sum_kernel(y_ref, got_y_ref, y_out, sum_ref):
    sum_ref[...] = y_ref[...] + got_y_ref[...]
    encode_rows(sum_ref, y_out)


def finish_q_kernel(own_ref, got_own_ref, got_ref, gq_out):
    rows = own_ref.shape[0]
    tail = got_ref[rows : rows + TAIL, :].astype(jnp.int32).astype(F32)
    own_tail = got_own_ref[rows:, :].astype(jnp.int32).astype(F32)
    for b in range(rows // BLK):
        at = slice(b * BLK, (b + 1) * BLK)
        own = own_ref[at, :] + decode(got_own_ref[at, :], own_tail[b : b + 1, :])
        gq_out[at, :] = own + decode(got_ref[at, :], tail[b : b + 1, :])


def finish_v_kernel(term_ref, *refs):
    got_terms, (gv_out, gd_out) = refs[:-2], refs[-2:]
    total = term_ref[...]
    dim = total.shape[0]
    for got in got_terms:
        tail = got[dim:, :].astype(jnp.int32).astype(F32)
        total = total + decode(got[0:dim, :], tail[0:1, :])
    local_v = gv_out.shape[0]
    gv_out[...] = total[:, :local_v].T
    gd_out[...] = total[:, local_v:].T


def body(queries, vectors, decoded, mask):
    rows, dim = queries.shape
    local_v = vectors.shape[0]
    blocks = mask.shape[0]
    n = lax.axis_size("qry")
    chunks = n // 4
    wide = 2 * local_v
    scale = 1.0 / math.sqrt(local_v * n)
    pad = -(-blocks // 16) * 16

    def swap(x, bit):
        return lax.ppermute(x, "qry", [(i, i ^ bit) for i in range(n)])

    q_y = swap(queries, 2)
    q_c = swap(queries, 1)
    q, vd, flags = pl.pallas_call(
        pack_kernel,
        out_shape=tuple(jax.ShapeDtypeStruct((r, dim), BF16) for r in (rows, wide, pad)),
        in_specs=[HBM] * 4,
        out_specs=(VMEM,) * 3,
        scratch_shapes=[pltpu.VMEM(mask.shape, mask.dtype), pltpu.SemaphoreType.DMA((4,))],
        compiler_params=params(8),
        name="pack",
    )(*[pltpu.with_memory_space_constraint(x, pltpu.HBM) for x in (queries, vectors, decoded, mask)])
    row_out = jax.ShapeDtypeStruct((rows, dim), F32)
    quarter = chunks // 4
    groups = [tuple(range(g * quarter, (g + 1) * quarter)) for g in range(4)]
    half = 2 * quarter

    def add(sets, which, gqs, gvs, name, table=None, row0=0, flags=None, send=(), code_last=False,
            weight=1):
        group = sum((groups[g] for g in which), ())
        return grads(
            sets, [vds[s] for s in group], group, chunks, rows, local_v, scale,
            table, row0, flags, gqs, gvs, send, code_last, name, weight,
        )

    flags_c = swap(flags, 1)
    vds = [vd] + [swap(vd, 4 * s) for s in range(1, chunks)]
    own = [q, q_c]
    near, far = tuple(range(1, half)), tuple(range(half, chunks))
    gq_o, gv0, (table, flags) = add(own, [0], None, None, "own_0", flags=[flags, flags_c])
    flags = swap(flags, 2)
    gq_o, gv1, _ = add(own, [1], gq_o, None, "own_1", table, weight=MEDIUM)
    q_y, gv1 = lax.optimization_barrier((q_y, gv1))
    q_yc = swap(q_y, 1)
    gq_y, gv01, (table_y,) = add([q_y], [0, 1], None, gv0 + gv1, "y_01", flags=[flags], weight=HEAVY)
    gq_yc, gv01, _ = add([q_yc], [0, 1], None, gv01, "yc_01", table_y, pad, send=near)
    gq_yc, gv01, late = lax.optimization_barrier((gq_yc, gv01, vds[half:][::-1]))
    vds[half:] = late[::-1]
    gq_yc, gv23, _ = add([q_yc], [2, 3], gq_yc, None, "yc_23", table_y, pad)
    got_y = swap(gq_yc[0], 1)
    gq_y, gv23, _ = add([q_y], [2, 3], gq_y, gv23, "y_23", table_y)
    gq_o, gv23, _ = add(own, [2, 3], gq_o, gv23, "own_23", table, send=far, code_last=True)
    got_y, gv01, gv23 = lax.optimization_barrier((got_y, gv01, gv23))
    gq_message = pl.pallas_call(
        core_sum_kernel,
        out_shape=jax.ShapeDtypeStruct((rows + 2 * TAIL, dim), I16),
        in_specs=[VMEM] * 2,
        out_specs=VMEM,
        scratch_shapes=[pltpu.VMEM((rows, dim), F32)],
        compiler_params=params(16),
        name="core_sum",
    )(gq_y[0], got_y)
    gq_own, gq_c = gq_o
    got_own = swap(gq_c, 1)
    term, *messages = gv01 + gv23
    got_message = swap(gq_message, 2)
    order = sorted(range(1, chunks), key=lambda s: (s < half, s))
    got_terms = [swap(messages[s - 1], 4 * s) for s in order]
    grad_q = pl.pallas_call(
        finish_q_kernel,
        out_shape=row_out,
        in_specs=[VMEM] * 3,
        out_specs=VMEM,
        compiler_params=params(16),
        name="finish_q",
    )(gq_own, got_own, got_message)
    grad_q, term = lax.optimization_barrier((grad_q, term))
    vec_out = jax.ShapeDtypeStruct((local_v, dim), F32)
    grad_v, grad_d = pl.pallas_call(
        finish_v_kernel,
        out_shape=(vec_out, vec_out),
        in_specs=[VMEM] * chunks,
        out_specs=(VMEM,) * 2,
        compiler_params=params(16),
        name="finish_v",
    )(term, *got_terms)
    return grad_q, grad_v, grad_d


def solution(mesh):
    placed = P(("groups", "qry"), None)
    return jax.shard_map(
        body,
        mesh=mesh,
        in_specs=(placed,) * 4,
        out_specs=(placed,) * 3,
        check_vma=False,
    )
```

```python
import math

import jax
import jax.numpy as jnp
from jax import lax
from jax.experimental import pallas as pl
from jax.experimental.pallas import tpu as pltpu
from jax.sharding import PartitionSpec as P

BLK = 256
LOG2E = 1.4426950408889634
LEVELS = 32000.0
TAIL = 16
HEAVY = 1 << 14
VMEM = pl.BlockSpec(memory_space=pltpu.VMEM)
HBM = pl.BlockSpec(memory_space=pltpu.HBM)
F32 = jnp.float32
BF16 = jnp.bfloat16
I16 = jnp.int16


def params(mib):
    return pltpu.CompilerParams(vmem_limit_bytes=mib << 20)


def cost(flops, nbytes):
    return pl.CostEstimate(flops=flops, bytes_accessed=nbytes, transcendentals=0)


def encode(x):
    top = jnp.max(jnp.abs(x), axis=0, keepdims=True)
    exponent = jnp.ceil(jnp.log2(jnp.maximum(top, 1e-30)))
    scaled = jnp.round(x * (jnp.exp2(-exponent) * LEVELS))
    return scaled.astype(jnp.int32).astype(I16), exponent


def decode(x, exponent):
    return x.astype(jnp.int32).astype(F32) * (jnp.exp2(exponent) * (1.0 / LEVELS))


def tail_of(exponents):
    rows = jnp.concatenate(exponents, axis=0)
    rest = jnp.zeros((TAIL - rows.shape[0], rows.shape[1]), F32)
    return jnp.concatenate([rows, rest], axis=0).astype(jnp.int32).astype(I16)


def encode_rows(x_ref, out_ref):
    rows = x_ref.shape[0]
    exponents = []
    for r in range(0, rows, BLK):
        code, exponent = encode(x_ref[r : r + BLK, :])
        out_ref[r : r + BLK, :] = code
        exponents.append(exponent)
    out_ref[rows : rows + TAIL, :] = tail_of(exponents)
    if out_ref.shape[0] > rows + TAIL:
        rest = (out_ref.shape[0] - rows - TAIL, out_ref.shape[1])
        out_ref[rows + TAIL :, :] = jnp.zeros(rest, I16)


def pack_kernel(q_hbm, v_hbm, d_hbm, m_hbm, qm_ref, far_ref, vd_ref, m_ref, sems):
    rows = q_hbm.shape[0]
    local_v = v_hbm.shape[0]
    copies = [
        pltpu.make_async_copy(m_hbm, m_ref, sems.at[0]),
        pltpu.make_async_copy(v_hbm, vd_ref.at[pl.ds(0, local_v)], sems.at[1]),
        pltpu.make_async_copy(d_hbm, vd_ref.at[pl.ds(local_v, local_v)], sems.at[2]),
        pltpu.make_async_copy(q_hbm, far_ref.at[pl.ds(0, rows)], sems.at[3]),
        pltpu.make_async_copy(q_hbm, qm_ref.at[pl.ds(0, rows)], sems.at[4]),
    ]
    for copy in copies:
        copy.start()
    copies[0].wait()
    blocks, cols = m_ref.shape
    pad, lanes = qm_ref.shape[0] - rows, qm_ref.shape[1]
    flags = jnp.concatenate([m_ref[...].astype(F32), jnp.zeros((blocks, lanes - cols), F32)], axis=1)
    flags = jnp.concatenate([flags, jnp.zeros((pad - blocks, lanes), F32)], axis=0)
    qm_ref[rows:, :] = flags.astype(BF16)
    far_ref[rows : rows + pad, :] = flags.astype(BF16)
    far_ref[rows + pad :, :] = flags.astype(BF16)
    for copy in copies[1:]:
        copy.wait()


def live_table(flags, chunks, local_v, scale):
    me = lax.axis_index("qry")
    lanes = flags.shape[1]
    rows = lax.broadcasted_iota(jnp.int32, (lanes, 128), 0)
    cols = [(jnp.bitwise_xor(me, 4 * s) * local_v) // BLK for s in range(chunks)]
    onehot = jnp.concatenate([(rows == col).astype(F32) for col in cols], axis=1)
    return jnp.dot(flags, onehot.astype(BF16), preferred_element_type=F32) * (-2.0 * scale)


def tile_weights(q, w, live, chunks, local_v):
    wide = 2 * local_v
    both = lax.dot_general(q, w, (((1,), (1,)), ((), ())), preferred_element_type=F32)
    row_blocks = []
    for b in range(q.shape[0] // BLK):
        weights = []
        for c in range(chunks):
            score = both[b * BLK : (b + 1) * BLK, c * wide : c * wide + local_v]
            error = score - both[b * BLK : (b + 1) * BLK, c * wide + local_v : (c + 1) * wide]
            sig = 1.0 / (1.0 + jnp.exp2(score * (-LOG2E)))
            neg = (error * live(b, c)) * sig
            pos = neg * (error * (0.5 * sig - 0.5) - 1.0)
            weights += [pos.astype(BF16), neg.astype(BF16)]
        row_blocks.append(jnp.concatenate(weights, axis=1))
    return jnp.concatenate(row_blocks, axis=0)


def grads(sets, vds, group, chunks, rows, local_v, scale, table, gqs, gvs, send, code_last, name, weight):
    k, m = len(sets), len(vds)
    dim = sets[0].shape[1]
    pad = -(-(rows // BLK) // 16) * 16
    wide = 2 * local_v
    part = min(m, 4)
    height = 2 * BLK if rows % (2 * BLK) == 0 else BLK
    fresh = table is None

    def kernel(*refs):
        qm_refs, refs = refs[:k], refs[k:]
        vd_refs, refs = refs[:m], refs[m:]
        gq_ins, gv_ins = None, None
        if not fresh:
            table_ref, refs = refs[0], refs[1:]
        if gqs is not None:
            gq_ins, refs = refs[:k], refs[k:]
        if gvs is not None:
            gv_ins, refs = refs[:m], refs[m:]
        gq_refs, refs = refs[:k], refs[k:]
        gv_outs, refs = refs[:m], refs[m:]
        if fresh:
            table_ref, refs = refs[0], refs[1:]
            for t in range(k):
                table = live_table(qm_refs[t][rows : rows + pad, :], chunks, local_v, scale)
                for s in range(chunks):
                    table_ref[s, t * pad : (t + 1) * pad, :] = table[:, s * 128 : (s + 1) * 128]
        gv_ref, w_ref, last_ref = refs
        for s in range(m):
            w_ref[s * wide : (s + 1) * wide, :] = vd_refs[s][...]
            gv_ref[:, s * wide : (s + 1) * wide] = (
                jnp.zeros((dim, wide), F32) if gv_ins is None else gv_ins[s][...]
            )
        outs = [*gq_refs[: k - 1], last_ref if code_last else gq_refs[k - 1]]

        def tile(t, r0, first):
            def live(b, c):
                s = group[first + c]
                return table_ref[s, pl.ds(t * pad + r0 // BLK + b, 1), :]

            w = w_ref[first * wide : (first + part) * wide, :]
            weights = tile_weights(qm_refs[t][pl.ds(r0, height), :], w, live, part, local_v)
            gq = jnp.dot(weights, w, preferred_element_type=F32)
            if first > 0:
                gq = gq + outs[t][pl.ds(r0, height), :]
            elif gq_ins is not None:
                gq = gq + gq_ins[t][pl.ds(r0, height), :]
            outs[t][pl.ds(r0, height), :] = gq
            return weights

        if m <= 4:
            weights = [tile(t, r0, 0) for t in range(k) for r0 in range(0, rows, height)]
            q = jnp.concatenate([ref[0:rows, :] for ref in qm_refs], axis=0)
            gv_ref[...] += jnp.dot(
                q.T, jnp.concatenate(weights, axis=0), preferred_element_type=F32
            )
        else:
            for t in range(k):
                for first in range(0, m, part):

                    def step(i, carry, t=t, first=first):
                        r0 = pl.multiple_of(i * height, height)
                        weights = tile(t, r0, first)
                        q = qm_refs[t][pl.ds(r0, height), :]
                        gv_ref[:, first * wide : (first + part) * wide] += jnp.dot(
                            q.T, weights, preferred_element_type=F32
                        )
                        return carry

                    lax.fori_loop(0, rows // height, step, 0)
        if code_last:
            encode_rows(last_ref, gq_refs[k - 1])
        for s in range(m):
            term = gv_ref[:, s * wide : (s + 1) * wide]
            if group[s] in send:
                code, exponent = encode(term)
                gv_outs[s][0:dim, :] = code
                gv_outs[s][dim:, :] = tail_of([exponent])
            else:
                gv_outs[s][...] = term

    operands = [*sets, *vds, *([] if fresh else [table]), *(gqs or []), *(gvs or [])]
    outs = [jax.ShapeDtypeStruct((rows, dim), F32)] * k + [
        jax.ShapeDtypeStruct((dim + TAIL, wide), I16)
        if s in send
        else jax.ShapeDtypeStruct((dim, wide), F32)
        for s in group
    ]
    if code_last:
        outs[k - 1] = jax.ShapeDtypeStruct((rows + TAIL, dim), I16)
    if fresh:
        outs.append(jax.ShapeDtypeStruct((chunks, k * pad, 128), F32))
    res = pl.pallas_call(
        kernel,
        out_shape=tuple(outs),
        in_specs=[VMEM] * len(operands),
        out_specs=(VMEM,) * len(outs),
        scratch_shapes=[
            pltpu.VMEM((dim, m * wide), F32),
            pltpu.VMEM((m * wide, dim), BF16),
            pltpu.VMEM((rows if code_last else 8, dim), F32),
        ],
        compiler_params=params(32),
        cost_estimate=cost(weight * k * rows * m * wide, 1 << 10),
        name=name,
    )(*operands)
    return list(res[:k]), list(res[k : k + m]), res[-1] if fresh else table


def core_sum_kernel(y_ref, got_y_ref, y_out, sum_ref):
    sum_ref[...] = y_ref[...] + got_y_ref[...]
    encode_rows(sum_ref, y_out)


def finish_q_kernel(own_ref, got_own_ref, got_ref, gq_out):
    rows = own_ref.shape[0]
    tail = got_ref[rows : rows + TAIL, :].astype(jnp.int32).astype(F32)
    own_tail = got_own_ref[rows:, :].astype(jnp.int32).astype(F32)
    for b in range(rows // BLK):
        at = slice(b * BLK, (b + 1) * BLK)
        own = own_ref[at, :] + decode(got_own_ref[at, :], own_tail[b : b + 1, :])
        gq_out[at, :] = own + decode(got_ref[at, :], tail[b : b + 1, :])


def finish_v_kernel(term_ref, *refs):
    got_terms, (gv_out, gd_out) = refs[:-2], refs[-2:]
    total = term_ref[...]
    dim = total.shape[0]
    for got in got_terms:
        tail = got[dim:, :].astype(jnp.int32).astype(F32)
        total = total + decode(got[0:dim, :], tail[0:1, :])
    local_v = gv_out.shape[0]
    gv_out[...] = total[:, :local_v].T
    gd_out[...] = total[:, local_v:].T


def body(queries, vectors, decoded, mask):
    rows, dim = queries.shape
    local_v = vectors.shape[0]
    blocks = mask.shape[0]
    n = lax.axis_size("qry")
    chunks = n // 4
    wide = 2 * local_v
    scale = 1.0 / math.sqrt(local_v * n)
    pad = -(-blocks // 16) * 16

    def swap(x, bit):
        return lax.ppermute(x, "qry", [(i, i ^ bit) for i in range(n)])

    qm, qm_far, vd = pl.pallas_call(
        pack_kernel,
        out_shape=(
            jax.ShapeDtypeStruct((rows + pad, dim), BF16),
            jax.ShapeDtypeStruct((rows + 2 * pad, dim), BF16),
            jax.ShapeDtypeStruct((wide, dim), BF16),
        ),
        in_specs=[HBM] * 4,
        out_specs=(VMEM,) * 3,
        scratch_shapes=[pltpu.VMEM(mask.shape, mask.dtype), pltpu.SemaphoreType.DMA((5,))],
        compiler_params=params(8),
        name="pack",
    )(*[pltpu.with_memory_space_constraint(x, pltpu.HBM) for x in (queries, vectors, decoded, mask)])
    row_out = jax.ShapeDtypeStruct((rows, dim), F32)
    quarter = chunks // 4
    groups = [tuple(range(g * quarter, (g + 1) * quarter)) for g in range(4)]
    half = 2 * quarter

    def add(sets, which, table, gqs, gvs, send, name, code_last=False, weight=1):
        group = sum((groups[g] for g in which), ())
        return grads(
            sets, [vds[s] for s in group], group, chunks, rows, local_v, scale,
            table, gqs, gvs, send, code_last, name, weight,
        )

    qm_y = swap(qm_far, 2)
    qm_c = swap(qm, 1)
    vds = [vd] + [swap(vd, 4 * s) for s in range(1, chunks)]
    own = [qm, qm_c]
    near, far = tuple(range(1, half)), tuple(range(half, chunks))
    gq_o, gv0, table = add(own, [0], None, None, None, (), "own_0", weight=0)
    gq_o, gv1, _ = add(own, [1], table, gq_o, None, (), "own_1", weight=0)
    qm_y, gv1 = lax.optimization_barrier((qm_y, gv1))
    qm_yc = swap(qm_y, 1)
    gq_y, gv01, table_y = add([qm_y], [0, 1], None, None, gv0 + gv1, (), "y_01", weight=HEAVY)
    gq_yc, gv01, table_yc = add([qm_yc], [0, 1], None, None, gv01, near, "yc_01")
    gq_yc, gv01, late = lax.optimization_barrier((gq_yc, gv01, vds[half:][::-1]))
    vds[half:] = late[::-1]
    gq_yc, gv23, _ = add([qm_yc], [2, 3], table_yc, gq_yc, None, (), "yc_23")
    got_y = swap(gq_yc[0], 1)
    gq_y, gv23, _ = add([qm_y], [2, 3], table_y, gq_y, gv23, (), "y_23")
    gq_o, gv23, _ = add(own, [2, 3], table, gq_o, gv23, far, "own_23", code_last=True)
    got_y, gv01, gv23 = lax.optimization_barrier((got_y, gv01, gv23))
    gq_message = pl.pallas_call(
        core_sum_kernel,
        out_shape=jax.ShapeDtypeStruct((rows + 2 * TAIL, dim), I16),
        in_specs=[VMEM] * 2,
        out_specs=VMEM,
        scratch_shapes=[pltpu.VMEM((rows, dim), F32)],
        compiler_params=params(16),
        name="core_sum",
    )(gq_y[0], got_y)
    gq_own, gq_c = gq_o
    got_own = swap(gq_c, 1)
    term, *messages = gv01 + gv23
    got_message = swap(gq_message, 2)
    order = sorted(range(1, chunks), key=lambda s: (s < half, s))
    got_terms = [swap(messages[s - 1], 4 * s) for s in order]
    grad_q = pl.pallas_call(
        finish_q_kernel,
        out_shape=row_out,
        in_specs=[VMEM] * 3,
        out_specs=VMEM,
        compiler_params=params(16),
        name="finish_q",
    )(gq_own, got_own, got_message)
    grad_q, term = lax.optimization_barrier((grad_q, term))
    vec_out = jax.ShapeDtypeStruct((local_v, dim), F32)
    grad_v, grad_d = pl.pallas_call(
        finish_v_kernel,
        out_shape=(vec_out, vec_out),
        in_specs=[VMEM] * chunks,
        out_specs=(VMEM,) * 2,
        compiler_params=params(16),
        name="finish_v",
    )(term, *got_terms)
    return grad_q, grad_v, grad_d


def solution(mesh):
    placed = P(("groups", "qry"), None)
    return jax.shard_map(
        body,
        mesh=mesh,
        in_specs=(placed,) * 4,
        out_specs=(placed,) * 3,
        check_vma=False,
    )
```

```python
import math

import jax
import jax.numpy as jnp
from jax import lax
from jax.experimental import pallas as pl
from jax.experimental.pallas import tpu as pltpu
from jax.sharding import PartitionSpec as P

BLK = 256
LOG2E = 1.4426950408889634
LEVELS = 32000.0
TAIL = 16
HEAVY = 1 << 14
VMEM = pl.BlockSpec(memory_space=pltpu.VMEM)
HBM = pl.BlockSpec(memory_space=pltpu.HBM)
F32 = jnp.float32
BF16 = jnp.bfloat16
I16 = jnp.int16


def params(mib):
    return pltpu.CompilerParams(vmem_limit_bytes=mib << 20)


def cost(flops, nbytes):
    return pl.CostEstimate(flops=flops, bytes_accessed=nbytes, transcendentals=0)


def encode(x):
    top = jnp.max(jnp.abs(x), axis=0, keepdims=True)
    exponent = jnp.ceil(jnp.log2(jnp.maximum(top, 1e-30)))
    scaled = jnp.round(x * (jnp.exp2(-exponent) * LEVELS))
    return scaled.astype(jnp.int32).astype(I16), exponent


def decode(x, exponent):
    return x.astype(jnp.int32).astype(F32) * (jnp.exp2(exponent) * (1.0 / LEVELS))


def tail_of(exponents):
    rows = jnp.concatenate(exponents, axis=0)
    rest = jnp.zeros((TAIL - rows.shape[0], rows.shape[1]), F32)
    return jnp.concatenate([rows, rest], axis=0).astype(jnp.int32).astype(I16)


def encode_rows(x_ref, out_ref):
    rows = x_ref.shape[0]
    exponents = []
    for r in range(0, rows, BLK):
        code, exponent = encode(x_ref[r : r + BLK, :])
        out_ref[r : r + BLK, :] = code
        exponents.append(exponent)
    out_ref[rows : rows + TAIL, :] = tail_of(exponents)
    if out_ref.shape[0] > rows + TAIL:
        rest = (out_ref.shape[0] - rows - TAIL, out_ref.shape[1])
        out_ref[rows + TAIL :, :] = jnp.zeros(rest, I16)


def pack_kernel(q_hbm, v_hbm, d_hbm, m_hbm, qm_ref, far_ref, vd_ref, m_ref, sems):
    rows = q_hbm.shape[0]
    local_v = v_hbm.shape[0]
    copies = [
        pltpu.make_async_copy(m_hbm, m_ref, sems.at[0]),
        pltpu.make_async_copy(v_hbm, vd_ref.at[pl.ds(0, local_v)], sems.at[1]),
        pltpu.make_async_copy(d_hbm, vd_ref.at[pl.ds(local_v, local_v)], sems.at[2]),
        pltpu.make_async_copy(q_hbm, far_ref.at[pl.ds(0, rows)], sems.at[3]),
        pltpu.make_async_copy(q_hbm, qm_ref.at[pl.ds(0, rows)], sems.at[4]),
    ]
    for copy in copies:
        copy.start()
    copies[0].wait()
    blocks, cols = m_ref.shape
    pad, lanes = qm_ref.shape[0] - rows, qm_ref.shape[1]
    flags = jnp.concatenate([m_ref[...].astype(F32), jnp.zeros((blocks, lanes - cols), F32)], axis=1)
    flags = jnp.concatenate([flags, jnp.zeros((pad - blocks, lanes), F32)], axis=0)
    qm_ref[rows:, :] = flags.astype(BF16)
    far_ref[rows : rows + pad, :] = flags.astype(BF16)
    far_ref[rows + pad :, :] = flags.astype(BF16)
    for copy in copies[1:]:
        copy.wait()


def live_table(flags, chunks, local_v, scale):
    me = lax.axis_index("qry")
    lanes = flags.shape[1]
    rows = lax.broadcasted_iota(jnp.int32, (lanes, 128), 0)
    cols = [(jnp.bitwise_xor(me, 4 * s) * local_v) // BLK for s in range(chunks)]
    onehot = jnp.concatenate([(rows == col).astype(F32) for col in cols], axis=1)
    return jnp.dot(flags, onehot.astype(BF16), preferred_element_type=F32) * (-2.0 * scale)


def tile_weights(q, w, live, chunks, local_v):
    wide = 2 * local_v
    both = lax.dot_general(q, w, (((1,), (1,)), ((), ())), preferred_element_type=F32)
    row_blocks = []
    for b in range(q.shape[0] // BLK):
        weights = []
        for c in range(chunks):
            score = both[b * BLK : (b + 1) * BLK, c * wide : c * wide + local_v]
            error = score - both[b * BLK : (b + 1) * BLK, c * wide + local_v : (c + 1) * wide]
            sig = 1.0 / (1.0 + jnp.exp2(score * (-LOG2E)))
            neg = (error * live(b, c)) * sig
            pos = neg * (error * (0.5 * sig - 0.5) - 1.0)
            weights += [pos.astype(BF16), neg.astype(BF16)]
        row_blocks.append(jnp.concatenate(weights, axis=1))
    return jnp.concatenate(row_blocks, axis=0)


def grads(sets, vds, group, chunks, rows, local_v, scale, table, gqs, gvs, send, code_last, name, weight):
    k, m = len(sets), len(vds)
    dim = sets[0].shape[1]
    pad = -(-(rows // BLK) // 16) * 16
    wide = 2 * local_v
    part = min(m, 4)
    height = 2 * BLK if rows % (2 * BLK) == 0 else BLK
    fresh = table is None

    def kernel(*refs):
        qm_refs, refs = refs[:k], refs[k:]
        vd_refs, refs = refs[:m], refs[m:]
        gq_ins, gv_ins = None, None
        if not fresh:
            table_ref, refs = refs[0], refs[1:]
        if gqs is not None:
            gq_ins, refs = refs[:k], refs[k:]
        if gvs is not None:
            gv_ins, refs = refs[:m], refs[m:]
        gq_refs, refs = refs[:k], refs[k:]
        gv_outs, refs = refs[:m], refs[m:]
        if fresh:
            table_ref, refs = refs[0], refs[1:]
            for t in range(k):
                table = live_table(qm_refs[t][rows : rows + pad, :], chunks, local_v, scale)
                for s in range(chunks):
                    table_ref[s, t * pad : (t + 1) * pad, :] = table[:, s * 128 : (s + 1) * 128]
        gv_ref, w_ref, last_ref = refs
        for s in range(m):
            w_ref[s * wide : (s + 1) * wide, :] = vd_refs[s][...]
            gv_ref[:, s * wide : (s + 1) * wide] = (
                jnp.zeros((dim, wide), F32) if gv_ins is None else gv_ins[s][...]
            )
        outs = [*gq_refs[: k - 1], last_ref if code_last else gq_refs[k - 1]]

        def tile(t, r0, first):
            def live(b, c):
                s = group[first + c]
                return table_ref[s, pl.ds(t * pad + r0 // BLK + b, 1), :]

            w = w_ref[first * wide : (first + part) * wide, :]
            weights = tile_weights(qm_refs[t][pl.ds(r0, height), :], w, live, part, local_v)
            gq = jnp.dot(weights, w, preferred_element_type=F32)
            if first > 0:
                gq = gq + outs[t][pl.ds(r0, height), :]
            elif gq_ins is not None:
                gq = gq + gq_ins[t][pl.ds(r0, height), :]
            outs[t][pl.ds(r0, height), :] = gq
            return weights

        if m <= 4:
            weights = [tile(t, r0, 0) for t in range(k) for r0 in range(0, rows, height)]
            q = jnp.concatenate([ref[0:rows, :] for ref in qm_refs], axis=0)
            gv_ref[...] += jnp.dot(
                q.T, jnp.concatenate(weights, axis=0), preferred_element_type=F32
            )
        else:
            for t in range(k):
                for first in range(0, m, part):

                    def step(i, carry, t=t, first=first):
                        r0 = pl.multiple_of(i * height, height)
                        weights = tile(t, r0, first)
                        q = qm_refs[t][pl.ds(r0, height), :]
                        gv_ref[:, first * wide : (first + part) * wide] += jnp.dot(
                            q.T, weights, preferred_element_type=F32
                        )
                        return carry

                    lax.fori_loop(0, rows // height, step, 0)
        if code_last:
            encode_rows(last_ref, gq_refs[k - 1])
        for s in range(m):
            term = gv_ref[:, s * wide : (s + 1) * wide]
            if group[s] in send:
                code, exponent = encode(term)
                gv_outs[s][0:dim, :] = code[:, :local_v]
                gv_outs[s][dim : 2 * dim, :] = code[:, local_v:]
                gv_outs[s][2 * dim :, :] = tail_of([exponent[:, :local_v], exponent[:, local_v:]])
            else:
                gv_outs[s][...] = term

    operands = [*sets, *vds, *([] if fresh else [table]), *(gqs or []), *(gvs or [])]
    outs = [jax.ShapeDtypeStruct((rows, dim), F32)] * k + [
        jax.ShapeDtypeStruct((2 * dim + TAIL, local_v), I16)
        if s in send
        else jax.ShapeDtypeStruct((dim, wide), F32)
        for s in group
    ]
    if code_last:
        outs[k - 1] = jax.ShapeDtypeStruct((rows + TAIL, dim), I16)
    if fresh:
        outs.append(jax.ShapeDtypeStruct((chunks, k * pad, 128), F32))
    res = pl.pallas_call(
        kernel,
        out_shape=tuple(outs),
        in_specs=[VMEM] * len(operands),
        out_specs=(VMEM,) * len(outs),
        scratch_shapes=[
            pltpu.VMEM((dim, m * wide), F32),
            pltpu.VMEM((m * wide, dim), BF16),
            pltpu.VMEM((rows if code_last else 8, dim), F32),
        ],
        compiler_params=params(32),
        cost_estimate=cost(weight * k * rows * m * wide, 1 << 10),
        name=name,
    )(*operands)
    return list(res[:k]), list(res[k : k + m]), res[-1] if fresh else table


def core_sum_kernel(y_ref, got_y_ref, y_out, sum_ref):
    sum_ref[...] = y_ref[...] + got_y_ref[...]
    encode_rows(sum_ref, y_out)


def finish_q_kernel(own_ref, got_own_ref, got_ref, gq_out):
    rows = own_ref.shape[0]
    tail = got_ref[rows : rows + TAIL, :].astype(jnp.int32).astype(F32)
    own_tail = got_own_ref[rows:, :].astype(jnp.int32).astype(F32)
    for b in range(rows // BLK):
        at = slice(b * BLK, (b + 1) * BLK)
        own = own_ref[at, :] + decode(got_own_ref[at, :], own_tail[b : b + 1, :])
        gq_out[at, :] = own + decode(got_ref[at, :], tail[b : b + 1, :])


def finish_v_kernel(term_ref, *refs):
    got_terms, (gv_out, gd_out) = refs[:-2], refs[-2:]
    dim = term_ref.shape[0]
    local_v = gv_out.shape[0]
    tails = [got[2 * dim :, :].astype(jnp.int32).astype(F32) for got in got_terms]
    for part, out in enumerate((gv_out, gd_out)):
        total = term_ref[:, part * local_v : (part + 1) * local_v]
        for got, tail in zip(got_terms, tails):
            code = got[part * dim : (part + 1) * dim, :]
            total = total + decode(code, tail[part : part + 1, :])
        out[...] = total.T


def body(queries, vectors, decoded, mask):
    rows, dim = queries.shape
    local_v = vectors.shape[0]
    blocks = mask.shape[0]
    n = lax.axis_size("qry")
    chunks = n // 4
    wide = 2 * local_v
    scale = 1.0 / math.sqrt(local_v * n)
    pad = -(-blocks // 16) * 16

    def swap(x, bit):
        return lax.ppermute(x, "qry", [(i, i ^ bit) for i in range(n)])

    qm, qm_far, vd = pl.pallas_call(
        pack_kernel,
        out_shape=(
            jax.ShapeDtypeStruct((rows + pad, dim), BF16),
            jax.ShapeDtypeStruct((rows + 2 * pad, dim), BF16),
            jax.ShapeDtypeStruct((wide, dim), BF16),
        ),
        in_specs=[HBM] * 4,
        out_specs=(VMEM,) * 3,
        scratch_shapes=[pltpu.VMEM(mask.shape, mask.dtype), pltpu.SemaphoreType.DMA((5,))],
        compiler_params=params(8),
        name="pack",
    )(*[pltpu.with_memory_space_constraint(x, pltpu.HBM) for x in (queries, vectors, decoded, mask)])
    row_out = jax.ShapeDtypeStruct((rows, dim), F32)
    quarter = chunks // 4
    groups = [tuple(range(g * quarter, (g + 1) * quarter)) for g in range(4)]
    half = 2 * quarter

    def add(sets, which, table, gqs, gvs, send, name, code_last=False, weight=1):
        group = sum((groups[g] for g in which), ())
        return grads(
            sets, [vds[s] for s in group], group, chunks, rows, local_v, scale,
            table, gqs, gvs, send, code_last, name, weight,
        )

    qm_y = swap(qm_far, 2)
    qm_c = swap(qm, 1)
    vds = [vd] + [swap(vd, 4 * s) for s in range(1, chunks)]
    own = [qm, qm_c]
    near, far = tuple(range(1, half)), tuple(range(half, chunks))
    gq_o, gv0, table = add(own, [0], None, None, None, (), "own_0", weight=0)
    gq_o, gv1, _ = add(own, [1], table, gq_o, None, (), "own_1", weight=0)
    qm_y, gv1 = lax.optimization_barrier((qm_y, gv1))
    qm_yc = swap(qm_y, 1)
    gq_y, gv01, table_y = add([qm_y], [0, 1], None, None, gv0 + gv1, (), "y_01", weight=HEAVY)
    gq_yc, gv01, table_yc = add([qm_yc], [0, 1], None, None, gv01, near, "yc_01")
    gq_yc, gv01, late = lax.optimization_barrier((gq_yc, gv01, vds[half:][::-1]))
    vds[half:] = late[::-1]
    gq_yc, gv23, _ = add([qm_yc], [2, 3], table_yc, gq_yc, None, (), "yc_23")
    got_y = swap(gq_yc[0], 1)
    gq_y, gv23, _ = add([qm_y], [2, 3], table_y, gq_y, gv23, (), "y_23")
    gq_o, gv23, _ = add(own, [2, 3], table, gq_o, gv23, far, "own_23", code_last=True)
    got_y, gv01, gv23 = lax.optimization_barrier((got_y, gv01, gv23))
    gq_message = pl.pallas_call(
        core_sum_kernel,
        out_shape=jax.ShapeDtypeStruct((rows + 2 * TAIL, dim), I16),
        in_specs=[VMEM] * 2,
        out_specs=VMEM,
        scratch_shapes=[pltpu.VMEM((rows, dim), F32)],
        compiler_params=params(16),
        name="core_sum",
    )(gq_y[0], got_y)
    gq_own, gq_c = gq_o
    got_own = swap(gq_c, 1)
    term, *messages = gv01 + gv23
    got_message = swap(gq_message, 2)
    order = sorted(range(1, chunks), key=lambda s: (s < half, s))
    got_terms = [swap(messages[s - 1], 4 * s) for s in order]
    grad_q = pl.pallas_call(
        finish_q_kernel,
        out_shape=row_out,
        in_specs=[VMEM] * 3,
        out_specs=VMEM,
        compiler_params=params(16),
        name="finish_q",
    )(gq_own, got_own, got_message)
    grad_q, term = lax.optimization_barrier((grad_q, term))
    vec_out = jax.ShapeDtypeStruct((local_v, dim), F32)
    grad_v, grad_d = pl.pallas_call(
        finish_v_kernel,
        out_shape=(vec_out, vec_out),
        in_specs=[VMEM] * chunks,
        out_specs=(VMEM,) * 2,
        compiler_params=params(16),
        name="finish_v",
    )(term, *got_terms)
    return grad_q, grad_v, grad_d


def solution(mesh):
    placed = P(("groups", "qry"), None)
    return jax.shard_map(
        body,
        mesh=mesh,
        in_specs=(placed,) * 4,
        out_specs=(placed,) * 3,
        check_vma=False,
    )
```

```python
import math

import jax
import jax.numpy as jnp
from jax import lax
from jax.experimental import pallas as pl
from jax.experimental.pallas import tpu as pltpu
from jax.sharding import PartitionSpec as P

BLK = 256
LOG2E = 1.4426950408889634
LEVELS = 32000.0
TAIL = 16
HEAVY = 1 << 14
VMEM = pl.BlockSpec(memory_space=pltpu.VMEM)
HBM = pl.BlockSpec(memory_space=pltpu.HBM)
F32 = jnp.float32
BF16 = jnp.bfloat16
I16 = jnp.int16


def params(mib):
    return pltpu.CompilerParams(vmem_limit_bytes=mib << 20)


def cost(flops, nbytes):
    return pl.CostEstimate(flops=flops, bytes_accessed=nbytes, transcendentals=0)


def encode(x):
    top = jnp.max(jnp.abs(x), axis=0, keepdims=True)
    exponent = jnp.ceil(jnp.log2(jnp.maximum(top, 1e-30)))
    scaled = jnp.round(x * (jnp.exp2(-exponent) * LEVELS))
    return scaled.astype(jnp.int32).astype(I16), exponent


def decode(x, exponent):
    return x.astype(jnp.int32).astype(F32) * (jnp.exp2(exponent) * (1.0 / LEVELS))


def tail_of(exponents):
    rows = jnp.concatenate(exponents, axis=0)
    rest = jnp.zeros((TAIL - rows.shape[0], rows.shape[1]), F32)
    return jnp.concatenate([rows, rest], axis=0).astype(jnp.int32).astype(I16)


def encode_rows(x_ref, out_ref):
    rows = x_ref.shape[0]
    exponents = []
    for r in range(0, rows, BLK):
        code, exponent = encode(x_ref[r : r + BLK, :])
        out_ref[r : r + BLK, :] = code
        exponents.append(exponent)
    out_ref[rows : rows + TAIL, :] = tail_of(exponents)
    if out_ref.shape[0] > rows + TAIL:
        rest = (out_ref.shape[0] - rows - TAIL, out_ref.shape[1])
        out_ref[rows + TAIL :, :] = jnp.zeros(rest, I16)


def pack_kernel(q_hbm, v_hbm, d_hbm, m_hbm, qm_ref, far_ref, vd_ref, m_ref, sems):
    rows = q_hbm.shape[0]
    local_v = v_hbm.shape[0]
    copies = [
        pltpu.make_async_copy(m_hbm, m_ref, sems.at[0]),
        pltpu.make_async_copy(v_hbm, vd_ref.at[pl.ds(0, local_v)], sems.at[1]),
        pltpu.make_async_copy(d_hbm, vd_ref.at[pl.ds(local_v, local_v)], sems.at[2]),
        pltpu.make_async_copy(q_hbm, far_ref.at[pl.ds(0, rows)], sems.at[3]),
        pltpu.make_async_copy(q_hbm, qm_ref.at[pl.ds(0, rows)], sems.at[4]),
    ]
    for copy in copies:
        copy.start()
    copies[0].wait()
    blocks, cols = m_ref.shape
    pad, lanes = qm_ref.shape[0] - rows, qm_ref.shape[1]
    flags = jnp.concatenate([m_ref[...].astype(F32), jnp.zeros((blocks, lanes - cols), F32)], axis=1)
    flags = jnp.concatenate([flags, jnp.zeros((pad - blocks, lanes), F32)], axis=0)
    qm_ref[rows:, :] = flags.astype(BF16)
    far_ref[rows : rows + pad, :] = flags.astype(BF16)
    far_ref[rows + pad :, :] = flags.astype(BF16)
    for copy in copies[1:]:
        copy.wait()


def live_table(flags, chunks, local_v, scale):
    me = lax.axis_index("qry")
    lanes = flags.shape[1]
    rows = lax.broadcasted_iota(jnp.int32, (lanes, 128), 0)
    cols = [(jnp.bitwise_xor(me, 4 * s) * local_v) // BLK for s in range(chunks)]
    onehot = jnp.concatenate([(rows == col).astype(F32) for col in cols], axis=1)
    return jnp.dot(flags, onehot.astype(BF16), preferred_element_type=F32) * (-2.0 * scale)


def tile_weights(q, w, live, chunks, local_v):
    wide = 2 * local_v
    both = lax.dot_general(q, w, (((1,), (1,)), ((), ())), preferred_element_type=F32)
    row_blocks = []
    for b in range(q.shape[0] // BLK):
        weights = []
        for c in range(chunks):
            score = both[b * BLK : (b + 1) * BLK, c * wide : c * wide + local_v]
            error = score - both[b * BLK : (b + 1) * BLK, c * wide + local_v : (c + 1) * wide]
            sig = 1.0 / (1.0 + jnp.exp2(score * (-LOG2E)))
            neg = (error * live(b, c)) * sig
            pos = neg * (error * (0.5 * sig - 0.5) - 1.0)
            weights += [pos.astype(BF16), neg.astype(BF16)]
        row_blocks.append(jnp.concatenate(weights, axis=1))
    return jnp.concatenate(row_blocks, axis=0)


def grads(sets, vds, group, chunks, rows, local_v, scale, table, gqs, gvs, send, code_last, name, weight):
    k, m = len(sets), len(vds)
    dim = sets[0].shape[1]
    pad = -(-(rows // BLK) // 16) * 16
    wide = 2 * local_v
    part = min(m, 4)
    height = 2 * BLK if rows % (2 * BLK) == 0 else BLK
    fresh = table is None
    tables = [] if fresh else table
    place = [(i, j) for i, x in enumerate(tables) for j in range(0, x.shape[1], pad)]

    def kernel(*refs):
        qm_refs, refs = refs[:k], refs[k:]
        vd_refs, refs = refs[:m], refs[m:]
        gq_ins, gv_ins = None, None
        if not fresh:
            table_refs, refs = refs[: len(tables)], refs[len(tables) :]
        if gqs is not None:
            gq_ins, refs = refs[:k], refs[k:]
        if gvs is not None:
            gv_ins, refs = refs[:m], refs[m:]
        gq_refs, refs = refs[:k], refs[k:]
        gv_outs, refs = refs[:m], refs[m:]
        if fresh:
            table_ref, refs = refs[0], refs[1:]
            for t in range(k):
                table = live_table(qm_refs[t][rows : rows + pad, :], chunks, local_v, scale)
                for s in range(chunks):
                    table_ref[s, t * pad : (t + 1) * pad, :] = table[:, s * 128 : (s + 1) * 128]
        gv_ref, w_ref, last_ref = refs
        for s in range(m):
            w_ref[s * wide : (s + 1) * wide, :] = vd_refs[s][...]
            gv_ref[:, s * wide : (s + 1) * wide] = (
                jnp.zeros((dim, wide), F32) if gv_ins is None else gv_ins[s][...]
            )
        outs = [*gq_refs[: k - 1], last_ref if code_last else gq_refs[k - 1]]

        def tile(t, r0, first):
            def live(b, c):
                s = group[first + c]
                ref, row = (table_ref, t * pad) if fresh else (table_refs[place[t][0]], place[t][1])
                return ref[s, pl.ds(row + r0 // BLK + b, 1), :]

            w = w_ref[first * wide : (first + part) * wide, :]
            weights = tile_weights(qm_refs[t][pl.ds(r0, height), :], w, live, part, local_v)
            gq = jnp.dot(weights, w, preferred_element_type=F32)
            if first > 0:
                gq = gq + outs[t][pl.ds(r0, height), :]
            elif gq_ins is not None:
                gq = gq + gq_ins[t][pl.ds(r0, height), :]
            outs[t][pl.ds(r0, height), :] = gq
            return weights

        if m <= 4:
            weights = [tile(t, r0, 0) for t in range(k) for r0 in range(0, rows, height)]
            q = jnp.concatenate([ref[0:rows, :] for ref in qm_refs], axis=0)
            gv_ref[...] += jnp.dot(
                q.T, jnp.concatenate(weights, axis=0), preferred_element_type=F32
            )
        else:
            for t in range(k):
                for first in range(0, m, part):

                    def step(i, carry, t=t, first=first):
                        r0 = pl.multiple_of(i * height, height)
                        weights = tile(t, r0, first)
                        q = qm_refs[t][pl.ds(r0, height), :]
                        gv_ref[:, first * wide : (first + part) * wide] += jnp.dot(
                            q.T, weights, preferred_element_type=F32
                        )
                        return carry

                    lax.fori_loop(0, rows // height, step, 0)
        if code_last:
            encode_rows(last_ref, gq_refs[k - 1])
        for s in range(m):
            term = gv_ref[:, s * wide : (s + 1) * wide]
            if group[s] in send:
                code, exponent = encode(term)
                gv_outs[s][0:dim, :] = code[:, :local_v]
                gv_outs[s][dim : 2 * dim, :] = code[:, local_v:]
                gv_outs[s][2 * dim :, :] = tail_of([exponent[:, :local_v], exponent[:, local_v:]])
            else:
                gv_outs[s][...] = term

    operands = [*sets, *vds, *tables, *(gqs or []), *(gvs or [])]
    outs = [jax.ShapeDtypeStruct((rows, dim), F32)] * k + [
        jax.ShapeDtypeStruct((2 * dim + TAIL, local_v), I16)
        if s in send
        else jax.ShapeDtypeStruct((dim, wide), F32)
        for s in group
    ]
    if code_last:
        outs[k - 1] = jax.ShapeDtypeStruct((rows + TAIL, dim), I16)
    if fresh:
        outs.append(jax.ShapeDtypeStruct((chunks, k * pad, 128), F32))
    res = pl.pallas_call(
        kernel,
        out_shape=tuple(outs),
        in_specs=[VMEM] * len(operands),
        out_specs=(VMEM,) * len(outs),
        scratch_shapes=[
            pltpu.VMEM((dim, m * wide), F32),
            pltpu.VMEM((m * wide, dim), BF16),
            pltpu.VMEM((rows if code_last else 8, dim), F32),
        ],
        compiler_params=params(32),
        cost_estimate=cost(weight * k * rows * m * wide, 1 << 10),
        name=name,
    )(*operands)
    return list(res[:k]), list(res[k : k + m]), res[-1] if fresh else table


def core_sum_kernel(y_ref, got_y_ref, y_out, sum_ref):
    sum_ref[...] = y_ref[...] + got_y_ref[...]
    encode_rows(sum_ref, y_out)


def finish_q_kernel(own_ref, got_own_ref, got_ref, gq_out):
    rows = own_ref.shape[0]
    tail = got_ref[rows : rows + TAIL, :].astype(jnp.int32).astype(F32)
    own_tail = got_own_ref[rows:, :].astype(jnp.int32).astype(F32)
    for b in range(rows // BLK):
        at = slice(b * BLK, (b + 1) * BLK)
        own = own_ref[at, :] + decode(got_own_ref[at, :], own_tail[b : b + 1, :])
        gq_out[at, :] = own + decode(got_ref[at, :], tail[b : b + 1, :])


def finish_v_kernel(term_ref, *refs):
    got_terms, (gv_out, gd_out) = refs[:-2], refs[-2:]
    dim = term_ref.shape[0]
    local_v = gv_out.shape[0]
    tails = [got[2 * dim :, :].astype(jnp.int32).astype(F32) for got in got_terms]
    for part, out in enumerate((gv_out, gd_out)):
        total = term_ref[:, part * local_v : (part + 1) * local_v]
        for got, tail in zip(got_terms, tails):
            code = got[part * dim : (part + 1) * dim, :]
            total = total + decode(code, tail[part : part + 1, :])
        out[...] = total.T


def body(queries, vectors, decoded, mask):
    rows, dim = queries.shape
    local_v = vectors.shape[0]
    blocks = mask.shape[0]
    n = lax.axis_size("qry")
    chunks = n // 4
    wide = 2 * local_v
    scale = 1.0 / math.sqrt(local_v * n)
    pad = -(-blocks // 16) * 16

    def swap(x, bit):
        return lax.ppermute(x, "qry", [(i, i ^ bit) for i in range(n)])

    qm, qm_far, vd = pl.pallas_call(
        pack_kernel,
        out_shape=(
            jax.ShapeDtypeStruct((rows + pad, dim), BF16),
            jax.ShapeDtypeStruct((rows + 2 * pad, dim), BF16),
            jax.ShapeDtypeStruct((wide, dim), BF16),
        ),
        in_specs=[HBM] * 4,
        out_specs=(VMEM,) * 3,
        scratch_shapes=[pltpu.VMEM(mask.shape, mask.dtype), pltpu.SemaphoreType.DMA((5,))],
        compiler_params=params(8),
        name="pack",
    )(*[pltpu.with_memory_space_constraint(x, pltpu.HBM) for x in (queries, vectors, decoded, mask)])
    row_out = jax.ShapeDtypeStruct((rows, dim), F32)
    quarter = chunks // 4
    groups = [tuple(range(g * quarter, (g + 1) * quarter)) for g in range(4)]
    half = 2 * quarter

    def add(sets, which, table, gqs, gvs, send, name, code_last=False, weight=1):
        group = sum((groups[g] for g in which), ())
        return grads(
            sets, [vds[s] for s in group], group, chunks, rows, local_v, scale,
            table, gqs, gvs, send, code_last, name, weight,
        )

    qm_y = swap(qm_far, 2)
    qm_c = swap(qm, 1)
    vds = [vd] + [swap(vd, 4 * s) for s in range(1, chunks)]
    own = [qm, qm_c]
    near, far = tuple(range(1, half)), tuple(range(half, chunks))
    gq_o, gv0, table = add(own, [0], None, None, None, (), "own_0", weight=0)
    gq_o, gv1, _ = add(own, [1], [table], gq_o, None, (), "own_1", weight=0)
    qm_y, gv1 = lax.optimization_barrier((qm_y, gv1))
    qm_yc = swap(qm_y, 1)
    gq_y, gv01, table_y = add([qm_y], [0, 1], None, None, gv0 + gv1, (), "y_01", weight=HEAVY)
    gq_yc, gv01, table_yc = add([qm_yc], [0, 1], None, None, gv01, near, "yc_01")
    gq_yc, gv01, late = lax.optimization_barrier((gq_yc, gv01, vds[half:][::-1]))
    vds[half:] = late[::-1]
    gq_yc, gv23, _ = add([qm_yc], [2, 3], [table_yc], gq_yc, None, (), "yc_23")
    got_y = swap(gq_yc[0], 1)
    sums, gv23, _ = add(
        [qm_y, *own], [2, 3], [table_y, table], [gq_y[0], *gq_o], gv23, far, "last_23", code_last=True
    )
    gq_y, gq_o = sums[:1], sums[1:]
    got_y, gv01, gv23 = lax.optimization_barrier((got_y, gv01, gv23))
    gq_message = pl.pallas_call(
        core_sum_kernel,
        out_shape=jax.ShapeDtypeStruct((rows + 2 * TAIL, dim), I16),
        in_specs=[VMEM] * 2,
        out_specs=VMEM,
        scratch_shapes=[pltpu.VMEM((rows, dim), F32)],
        compiler_params=params(16),
        name="core_sum",
    )(gq_y[0], got_y)
    gq_own, gq_c = gq_o
    got_own = swap(gq_c, 1)
    term, *messages = gv01 + gv23
    got_message = swap(gq_message, 2)
    order = sorted(range(1, chunks), key=lambda s: (s < half, s))
    got_terms = [swap(messages[s - 1], 4 * s) for s in order]
    grad_q = pl.pallas_call(
        finish_q_kernel,
        out_shape=row_out,
        in_specs=[VMEM] * 3,
        out_specs=VMEM,
        compiler_params=params(16),
        name="finish_q",
    )(gq_own, got_own, got_message)
    grad_q, term = lax.optimization_barrier((grad_q, term))
    vec_out = jax.ShapeDtypeStruct((local_v, dim), F32)
    grad_v, grad_d = pl.pallas_call(
        finish_v_kernel,
        out_shape=(vec_out, vec_out),
        in_specs=[VMEM] * chunks,
        out_specs=(VMEM,) * 2,
        compiler_params=params(16),
        name="finish_v",
    )(term, *got_terms)
    return grad_q, grad_v, grad_d


def solution(mesh):
    placed = P(("groups", "qry"), None)
    return jax.shard_map(
        body,
        mesh=mesh,
        in_specs=(placed,) * 4,
        out_specs=(placed,) * 3,
        check_vma=False,
    )
```

```python
import math

import jax
import jax.numpy as jnp
from jax import lax
from jax.experimental import pallas as pl
from jax.experimental.pallas import tpu as pltpu
from jax.sharding import PartitionSpec as P

BLK = 256
LOG2E = 1.4426950408889634
LEVELS = 32000.0
TAIL = 16
HEAVY = 1 << 14
VMEM = pl.BlockSpec(memory_space=pltpu.VMEM)
HBM = pl.BlockSpec(memory_space=pltpu.HBM)
F32 = jnp.float32
BF16 = jnp.bfloat16
I16 = jnp.int16


def params(mib):
    return pltpu.CompilerParams(vmem_limit_bytes=mib << 20)


def cost(flops, nbytes):
    return pl.CostEstimate(flops=flops, bytes_accessed=nbytes, transcendentals=0)


def encode(x):
    top = jnp.max(jnp.abs(x), axis=0, keepdims=True)
    exponent = jnp.ceil(jnp.log2(jnp.maximum(top, 1e-30)))
    scaled = jnp.round(x * (jnp.exp2(-exponent) * LEVELS))
    return scaled.astype(jnp.int32).astype(I16), exponent


def decode(x, exponent):
    return x.astype(jnp.int32).astype(F32) * (jnp.exp2(exponent) * (1.0 / LEVELS))


def tail_of(exponents):
    rows = jnp.concatenate(exponents, axis=0)
    rest = jnp.zeros((TAIL - rows.shape[0], rows.shape[1]), F32)
    return jnp.concatenate([rows, rest], axis=0).astype(jnp.int32).astype(I16)


def encode_rows(x_ref, out_ref):
    rows = x_ref.shape[0]
    exponents = []
    for r in range(0, rows, BLK):
        code, exponent = encode(x_ref[r : r + BLK, :])
        out_ref[r : r + BLK, :] = code
        exponents.append(exponent)
    out_ref[rows : rows + TAIL, :] = tail_of(exponents)
    if out_ref.shape[0] > rows + TAIL:
        rest = (out_ref.shape[0] - rows - TAIL, out_ref.shape[1])
        out_ref[rows + TAIL :, :] = jnp.zeros(rest, I16)


def pack_kernel(q_hbm, v_hbm, d_hbm, m_hbm, qm_ref, far_ref, vd_ref, m_ref, sems):
    rows = q_hbm.shape[0]
    local_v = v_hbm.shape[0]
    copies = [
        pltpu.make_async_copy(m_hbm, m_ref, sems.at[0]),
        pltpu.make_async_copy(v_hbm, vd_ref.at[pl.ds(0, local_v)], sems.at[1]),
        pltpu.make_async_copy(d_hbm, vd_ref.at[pl.ds(local_v, local_v)], sems.at[2]),
        pltpu.make_async_copy(q_hbm, far_ref.at[pl.ds(0, rows)], sems.at[3]),
        pltpu.make_async_copy(q_hbm, qm_ref.at[pl.ds(0, rows)], sems.at[4]),
    ]
    for copy in copies:
        copy.start()
    copies[0].wait()
    blocks, cols = m_ref.shape
    pad, lanes = qm_ref.shape[0] - rows, qm_ref.shape[1]
    flags = jnp.concatenate([m_ref[...].astype(F32), jnp.zeros((blocks, lanes - cols), F32)], axis=1)
    flags = jnp.concatenate([flags, jnp.zeros((pad - blocks, lanes), F32)], axis=0)
    qm_ref[rows:, :] = flags.astype(BF16)
    far_ref[rows : rows + pad, :] = flags.astype(BF16)
    far_ref[rows + pad :, :] = flags.astype(BF16)
    for copy in copies[1:]:
        copy.wait()


def live_table(flags, chunks, local_v, scale):
    me = lax.axis_index("qry")
    lanes = flags.shape[1]
    rows = lax.broadcasted_iota(jnp.int32, (lanes, 128), 0)
    cols = [(jnp.bitwise_xor(me, 4 * s) * local_v) // BLK for s in range(chunks)]
    onehot = jnp.concatenate([(rows == col).astype(F32) for col in cols], axis=1)
    return jnp.dot(flags, onehot.astype(BF16), preferred_element_type=F32) * (-2.0 * scale)


def tile_weights(q, w, live, chunks, local_v):
    wide = 2 * local_v
    both = lax.dot_general(q, w, (((1,), (1,)), ((), ())), preferred_element_type=F32)
    row_blocks = []
    for b in range(q.shape[0] // BLK):
        weights = []
        for c in range(chunks):
            score = both[b * BLK : (b + 1) * BLK, c * wide : c * wide + local_v]
            error = score - both[b * BLK : (b + 1) * BLK, c * wide + local_v : (c + 1) * wide]
            sig = 1.0 / (1.0 + jnp.exp2(score * (-LOG2E)))
            neg = (error * live(b, c)) * sig
            pos = neg * (error * (0.5 * sig - 0.5) - 1.0)
            weights += [pos.astype(BF16), neg.astype(BF16)]
        row_blocks.append(jnp.concatenate(weights, axis=1))
    return jnp.concatenate(row_blocks, axis=0)


def grads(sets, vds, group, chunks, rows, local_v, scale, table, gqs, gvs, send, code_last, name, weight):
    k, m = len(sets), len(vds)
    dim = sets[0].shape[1]
    pad = -(-(rows // BLK) // 16) * 16
    wide = 2 * local_v
    part = min(m, 4)
    height = 2 * BLK if rows % (2 * BLK) == 0 else BLK
    fresh = table is None
    tables = [] if fresh else table
    place = [(i, j) for i, x in enumerate(tables) for j in range(0, x.shape[1], pad)]

    def kernel(*refs):
        qm_refs, refs = refs[:k], refs[k:]
        vd_refs, refs = refs[:m], refs[m:]
        gq_ins, gv_ins = None, None
        if not fresh:
            table_refs, refs = refs[: len(tables)], refs[len(tables) :]
        if gqs is not None:
            gq_ins, refs = refs[:k], refs[k:]
        if gvs is not None:
            gv_ins, refs = refs[:m], refs[m:]
        gq_refs, refs = refs[:k], refs[k:]
        gv_outs, refs = refs[:m], refs[m:]
        if fresh:
            table_ref, refs = refs[0], refs[1:]
            for t in range(k):
                table = live_table(qm_refs[t][rows : rows + pad, :], chunks, local_v, scale)
                for s in range(chunks):
                    table_ref[s, t * pad : (t + 1) * pad, :] = table[:, s * 128 : (s + 1) * 128]
        gv_ref, w_ref, last_ref = refs
        for s in range(m):
            w_ref[s * wide : (s + 1) * wide, :] = vd_refs[s][...]
            gv_ref[:, s * wide : (s + 1) * wide] = (
                jnp.zeros((dim, wide), F32) if gv_ins is None else gv_ins[s][...]
            )
        outs = [*gq_refs[: k - 1], last_ref if code_last else gq_refs[k - 1]]

        def tile(t, r0, first):
            def live(b, c):
                s = group[first + c]
                ref, row = (table_ref, t * pad) if fresh else (table_refs[place[t][0]], place[t][1])
                return ref[s, pl.ds(row + r0 // BLK + b, 1), :]

            w = w_ref[first * wide : (first + part) * wide, :]
            weights = tile_weights(qm_refs[t][pl.ds(r0, height), :], w, live, part, local_v)
            gq = jnp.dot(weights, w, preferred_element_type=F32)
            if first > 0:
                gq = gq + outs[t][pl.ds(r0, height), :]
            elif gq_ins is not None:
                gq = gq + gq_ins[t][pl.ds(r0, height), :]
            outs[t][pl.ds(r0, height), :] = gq
            return weights

        if m <= 4:
            weights = [tile(t, r0, 0) for t in range(k) for r0 in range(0, rows, height)]
            q = jnp.concatenate([ref[0:rows, :] for ref in qm_refs], axis=0)
            gv_ref[...] += jnp.dot(
                q.T, jnp.concatenate(weights, axis=0), preferred_element_type=F32
            )
        else:
            for t in range(k):
                for first in range(0, m, part):

                    def step(i, carry, t=t, first=first):
                        r0 = pl.multiple_of(i * height, height)
                        weights = tile(t, r0, first)
                        q = qm_refs[t][pl.ds(r0, height), :]
                        gv_ref[:, first * wide : (first + part) * wide] += jnp.dot(
                            q.T, weights, preferred_element_type=F32
                        )
                        return carry

                    lax.fori_loop(0, rows // height, step, 0)
        if code_last:
            encode_rows(last_ref, gq_refs[k - 1])
        for s in range(m):
            term = gv_ref[:, s * wide : (s + 1) * wide]
            if group[s] in send:
                code, exponent = encode(term)
                gv_outs[s][0:dim, :] = code[:, :local_v]
                gv_outs[s][dim : 2 * dim, :] = code[:, local_v:]
                gv_outs[s][2 * dim :, :] = tail_of([exponent[:, :local_v], exponent[:, local_v:]])
            else:
                gv_outs[s][...] = term

    operands = [*sets, *vds, *tables, *(gqs or []), *(gvs or [])]
    outs = [jax.ShapeDtypeStruct((rows, dim), F32)] * k + [
        jax.ShapeDtypeStruct((2 * dim + TAIL, local_v), I16)
        if s in send
        else jax.ShapeDtypeStruct((dim, wide), F32)
        for s in group
    ]
    if code_last:
        outs[k - 1] = jax.ShapeDtypeStruct((rows + TAIL, dim), I16)
    if fresh:
        outs.append(jax.ShapeDtypeStruct((chunks, k * pad, 128), F32))
    res = pl.pallas_call(
        kernel,
        out_shape=tuple(outs),
        in_specs=[VMEM] * len(operands),
        out_specs=(VMEM,) * len(outs),
        scratch_shapes=[
            pltpu.VMEM((dim, m * wide), F32),
            pltpu.VMEM((m * wide, dim), BF16),
            pltpu.VMEM((rows if code_last else 8, dim), F32),
        ],
        compiler_params=params(32),
        cost_estimate=cost(weight * k * rows * m * wide, 1 << 10),
        name=name,
    )(*operands)
    return list(res[:k]), list(res[k : k + m]), res[-1] if fresh else table


def core_sum_kernel(y_ref, got_y_ref, y_out, sum_ref):
    sum_ref[...] = y_ref[...] + got_y_ref[...]
    encode_rows(sum_ref, y_out)


def finish_q_kernel(own_ref, got_own_ref, got_ref, gq_out):
    rows = own_ref.shape[0]
    tail = got_ref[rows : rows + TAIL, :].astype(jnp.int32).astype(F32)
    own_tail = got_own_ref[rows:, :].astype(jnp.int32).astype(F32)
    for b in range(rows // BLK):
        at = slice(b * BLK, (b + 1) * BLK)
        own = own_ref[at, :] + decode(got_own_ref[at, :], own_tail[b : b + 1, :])
        gq_out[at, :] = own + decode(got_ref[at, :], tail[b : b + 1, :])


def finish_v_kernel(term_ref, *refs):
    got_terms, (gv_out, gd_out) = refs[:-2], refs[-2:]
    dim = term_ref.shape[0]
    local_v = gv_out.shape[0]
    tails = [got[2 * dim :, :].astype(jnp.int32).astype(F32) for got in got_terms]
    for part, out in enumerate((gv_out, gd_out)):
        total = term_ref[:, part * local_v : (part + 1) * local_v]
        for got, tail in zip(got_terms, tails):
            code = got[part * dim : (part + 1) * dim, :]
            total = total + decode(code, tail[part : part + 1, :])
        out[...] = total.T


def body(queries, vectors, decoded, mask):
    rows, dim = queries.shape
    local_v = vectors.shape[0]
    blocks = mask.shape[0]
    n = lax.axis_size("qry")
    chunks = n // 4
    wide = 2 * local_v
    scale = 1.0 / math.sqrt(local_v * n)
    pad = -(-blocks // 16) * 16

    def swap(x, bit):
        return lax.ppermute(x, "qry", [(i, i ^ bit) for i in range(n)])

    qm, qm_far, vd = pl.pallas_call(
        pack_kernel,
        out_shape=(
            jax.ShapeDtypeStruct((rows + pad, dim), BF16),
            jax.ShapeDtypeStruct((rows + 2 * pad, dim), BF16),
            jax.ShapeDtypeStruct((wide, dim), BF16),
        ),
        in_specs=[HBM] * 4,
        out_specs=(VMEM,) * 3,
        scratch_shapes=[pltpu.VMEM(mask.shape, mask.dtype), pltpu.SemaphoreType.DMA((5,))],
        compiler_params=params(8),
        name="pack",
    )(*[pltpu.with_memory_space_constraint(x, pltpu.HBM) for x in (queries, vectors, decoded, mask)])
    row_out = jax.ShapeDtypeStruct((rows, dim), F32)
    quarter = chunks // 4
    groups = [tuple(range(g * quarter, (g + 1) * quarter)) for g in range(4)]
    half = 2 * quarter

    def add(sets, which, table, gqs, gvs, send, name, code_last=False, weight=1):
        group = sum((groups[g] for g in which), ())
        return grads(
            sets, [vds[s] for s in group], group, chunks, rows, local_v, scale,
            table, gqs, gvs, send, code_last, name, weight,
        )

    qm_y = swap(qm_far, 2)
    qm_c = swap(qm, 1)
    vds = [vd] + [swap(vd, 4 * s) for s in range(1, chunks)]
    own = [qm, qm_c]
    near, far = tuple(range(1, half)), tuple(range(half, chunks))
    gq_o, gv0, table = add(own, [0], None, None, None, (), "own_0", weight=0)
    gq_o, gv1, _ = add(own, [1], [table], gq_o, None, (), "own_1", weight=0)
    qm_y, gv1 = lax.optimization_barrier((qm_y, gv1))
    qm_yc = swap(qm_y, 1)
    gq_y, gv01, table_y = add([qm_y], [0, 1], None, None, gv0 + gv1, (), "y_01", weight=HEAVY)
    empty = jnp.zeros((dim, wide), F32)
    gq_yc, gvs, _ = add(
        [qm_yc], [0, 1, 2, 3], None, None, gv01 + [empty] * (chunks - half), near, "yc"
    )
    gv01, gv23 = gvs[:half], gvs[half:]
    got_y = swap(gq_yc[0], 1)
    sums, gv23, _ = add(
        [qm_y, *own], [2, 3], [table_y, table], [gq_y[0], *gq_o], gv23, far, "last_23", code_last=True
    )
    gq_y, gq_o = sums[:1], sums[1:]
    got_y, gv01, gv23 = lax.optimization_barrier((got_y, gv01, gv23))
    gq_message = pl.pallas_call(
        core_sum_kernel,
        out_shape=jax.ShapeDtypeStruct((rows + 2 * TAIL, dim), I16),
        in_specs=[VMEM] * 2,
        out_specs=VMEM,
        scratch_shapes=[pltpu.VMEM((rows, dim), F32)],
        compiler_params=params(16),
        name="core_sum",
    )(gq_y[0], got_y)
    gq_own, gq_c = gq_o
    got_own = swap(gq_c, 1)
    term, *messages = gv01 + gv23
    got_message = swap(gq_message, 2)
    order = sorted(range(1, chunks), key=lambda s: (s < half, s))
    got_terms = [swap(messages[s - 1], 4 * s) for s in order]
    grad_q = pl.pallas_call(
        finish_q_kernel,
        out_shape=row_out,
        in_specs=[VMEM] * 3,
        out_specs=VMEM,
        compiler_params=params(16),
        name="finish_q",
    )(gq_own, got_own, got_message)
    grad_q, term = lax.optimization_barrier((grad_q, term))
    vec_out = jax.ShapeDtypeStruct((local_v, dim), F32)
    grad_v, grad_d = pl.pallas_call(
        finish_v_kernel,
        out_shape=(vec_out, vec_out),
        in_specs=[VMEM] * chunks,
        out_specs=(VMEM,) * 2,
        compiler_params=params(16),
        name="finish_v",
    )(term, *got_terms)
    return grad_q, grad_v, grad_d


def solution(mesh):
    placed = P(("groups", "qry"), None)
    return jax.shard_map(
        body,
        mesh=mesh,
        in_specs=(placed,) * 4,
        out_specs=(placed,) * 3,
        check_vma=False,
    )
```
